256 devices in a mesh: blk: 8 (over z), fft: 32 (over x, y, core).
Axes of the slice: x: 4, y: 4, z: 8, core: 2. Of those that a mesh axis runs over, the one named last changes fastest.
Arguments:
- tokens: bfloat16 [32768, 1024], P(('blk', 'fft')), may hold values from -6 to 6
- w_in: bfloat16 [1024, 1536], replicated, may hold values from -0.1875 to 0.1875
- conv_taps: float32 [3, 1536], replicated, may hold values from -3 to 3
- causal_taps: bfloat16 [32768, 512], P(('blk', 'fft')), may hold values from -0.0625 to 0.0625
- anticausal_taps: bfloat16 [32768, 512], P(('blk', 'fft')), may hold values from -0.0625 to 0.0625
- skip_gain: float32 [512], replicated, may hold values from 0.1 to 1.9
- w_out: bfloat16 [512, 1024], replicated, may hold values from -0.25 to 0.25
Outputs:
- mixed_out: bfloat16 [32768, 1024], P(('blk', 'fft'))
The draws below stay inside these ranges and needn't reach their ends.
All inputs are finite; a program needn't handle non-finite values.
Results may differ from the reference program's by a relative error of at most 0.013.
Values may be sent and summed in bfloat16 or wider, within the bound.
No kernel may reach another device: no remote copies, remote signals or barrier semaphores. Data moves between devices by JAX's collectives and lax.ppermute only.
A program may use at most 64 MiB of HBM per device.

```python
import jax
import jax.numpy as jnp

D = 1024
CH = 512
SEQ = 32768


def block_scale(stream_key, dims, split, smallest, largest):
    def one(dim, shards_of):
        draws = jax.random.uniform(jax.random.fold_in(jax.random.fold_in(stream_key, 6), dim), (shards_of,), jnp.float32, smallest / len(split), largest / len(split))
        return jnp.repeat(jnp.exp(draws), dims[dim] // shards_of).reshape((-1,) + (1,) * (len(dims) - dim - 1))

    factor_of = one(*split[0])
    for cut in split[1:]:
        factor_of = factor_of * one(*cut)
    return factor_of


def scatter_about(rng, dims, width, most, shards=(), kind=jnp.bfloat16):
    result = jax.random.normal(rng, dims, jnp.float32) * width
    if len(shards) > 0:
        result = block_scale(rng, dims, shards, -0.22, 0.18) * result
    return jnp.clip(result, min=-most, max=most).astype(kind)


def setup_inputs(seed: int = 0) -> dict:
    seeds = jax.random.split(jax.random.key(seed), 8)
    return {
        "tokens": scatter_about(seeds[0], (SEQ, D), 1.0, 6.0, ((0, 256),)),
        "w_in": scatter_about(seeds[1], (D, 3 * CH), D ** -0.5, 0.1875),
        "conv_taps": scatter_about(seeds[2], (3, 3 * CH), 0.6, 3.0, (), jnp.float32),
        "causal_taps": scatter_about(seeds[3], (SEQ, CH), (1.0 / (2 * SEQ) ** 0.5), 0.0625, ((0, 256),)),
        "anticausal_taps": scatter_about(seeds[4], (SEQ, CH), (1.0 / (2 * SEQ) ** 0.5), 0.0625, ((0, 256),)),
        "skip_gain": jnp.clip(1.0 + 0.18 * jax.random.normal(seeds[5], (CH,), jnp.float32), 0.1, 1.9),
        "w_out": scatter_about(seeds[6], (CH, D), CH ** -0.5, 0.25),
    }


def reference(tokens, w_in, conv_taps, causal_taps, anticausal_taps, skip_gain, w_out):
    proj = jnp.dot(tokens, w_in, preferred_element_type=jnp.float32).astype(jnp.bfloat16)
    framed = jnp.pad(proj.astype(jnp.float32), ((1, 1), (0, 0)))
    short = conv_taps[0] * framed[:-2] + conv_taps[1] * framed[1:-1] + conv_taps[2] * framed[2:]
    first = short[:, :CH]
    second = short[:, CH:2 * CH]
    value_part = short[:, 2 * CH:]
    signal = first * value_part
    position = jnp.arange(SEQ, dtype=jnp.int32)
    anticausal = jnp.where(position[:, None] > 0, anticausal_taps.astype(jnp.float32), 0.0)
    circular = jnp.concatenate([causal_taps.astype(jnp.float32), anticausal], axis=0)
    padded = jnp.concatenate([signal, jnp.zeros_like(signal)], axis=0)
    spectrum = jnp.fft.rfft(padded, axis=0) * jnp.fft.rfft(circular, axis=0)
    convolved = jnp.fft.irfft(spectrum, n=2 * SEQ, axis=0)[:SEQ]
    convolved = convolved + skip_gain * signal
    gated = (second * convolved).astype(jnp.bfloat16)
    return jnp.dot(gated, w_out, preferred_element_type=jnp.float32).astype(jnp.bfloat16)
```

```python
import math

import jax
import jax.numpy as jnp
import numpy as np
from jax import lax
from jax.experimental import pallas as pl
from jax.experimental.pallas import tpu as pltpu
from jax.sharding import PartitionSpec as P

AXES = ("blk", "fft")
F32 = jnp.float32
BF16 = jnp.bfloat16


def tables(blocks, tok):
    length = 2 * blocks * tok
    half = np.arange(blocks) + 0.5
    ang = 2 * math.pi * np.outer(half, np.arange(2 * blocks)) / (2 * blocks)
    fore = np.concatenate([np.cos(ang), -np.sin(ang)], 0)
    back = np.concatenate([fore[:blocks, :blocks].T, fore[blocks:, :blocks].T], 1) * (2 / length)
    fore[:, blocks:] *= -1
    twist = 2 * math.pi * np.outer(half, np.arange(tok)) / length
    inner = 2 * math.pi * np.outer(np.arange(tok), np.arange(tok)) / tok
    c, s = np.cos(inner), np.sin(inner)
    q_fore = np.block([[c, -s], [s, c]])
    q_back = np.block([[c, s], [-s, c]])
    small = [jnp.asarray(a, BF16) for a in (fore, q_fore, q_back, back)]
    return small + [jnp.asarray(np.cos(twist), F32), jnp.asarray(np.sin(twist), F32)]


def dot(a, b):
    return jnp.dot(a, b, preferred_element_type=F32)


def filter_kernel(causal_ref, anti_ref, out_ref, buf, wide):
    channels = causal_ref.shape[1]
    half = channels // 2
    for a, ref in enumerate((causal_ref, anti_ref)):
        buf[...] = ref[...].astype(F32).T
        for c in range(2):
            wide[pl.ds(2 * a + c, half, stride=4), :] = buf[pl.ds(c, half, stride=2), :]
    out_ref[...] = wide[...].astype(BF16)


def front_kernel(proj_ref, edge_ref, taps_ref, skip_ref, sig_ref, second_ref, direct_ref):
    rows = proj_ref.shape[0]
    channels = proj_ref.shape[1] // 3
    row = lax.broadcasted_iota(jnp.int32, (rows, channels), 0)

    def short(i):
        cols = slice(i * channels, (i + 1) * channels)
        mid = proj_ref[:, cols].astype(F32)
        edge = edge_ref[:, cols].astype(F32)
        up = jnp.where(row == 0, edge[0:1], pltpu.roll(mid, 1, 0))
        down = jnp.where(row == rows - 1, edge[1:2], pltpu.roll(mid, rows - 1, 0))
        return taps_ref[0:1, cols] * up + taps_ref[1:2, cols] * mid + taps_ref[2:3, cols] * down

    signal = short(0) * short(2)
    sig_ref[...] = signal.T.astype(BF16)
    second_ref[...] = short(1).T
    direct_ref[...] = (skip_ref[...] * signal).T


def conv_kernel(sig_ref, filt_ref, fore_ref, qf_ref, qb_ref, back_ref, cos_ref, sin_ref, out_ref, buf, wide):
    blocks = sig_ref.shape[0] // 2
    tok = sig_ref.shape[1]
    cos, sin = cos_ref[...], sin_ref[...]

    def spectrum(b):
        parts = []
        for c in range(2):
            lanes = slice(c * tok, (c + 1) * tok)
            re, im = b[:blocks, lanes], b[blocks:, lanes]
            parts.append(jnp.concatenate([re * cos + im * sin, im * cos - re * sin], 1))
        return dot(jnp.concatenate(parts, 0).astype(BF16), qf_ref[...])

    wide[...] = filt_ref[...].astype(F32)
    taps = [
        jnp.concatenate([wide[pl.ds(2 * a + c, blocks, stride=4), :] for c in range(2)], 1)
        for a in range(2)
    ]
    place = lax.broadcasted_iota(jnp.int32, (blocks, 2 * tok), 0)
    lane = lax.broadcasted_iota(jnp.int32, (blocks, 2 * tok), 1)
    taps[1] = jnp.where((place == 0) & (lane % tok == 0), 0.0, taps[1])
    f = spectrum(dot(fore_ref[...], jnp.concatenate(taps, 0).astype(BF16)))

    buf[...] = sig_ref[...].astype(F32)
    x = jnp.concatenate([buf[pl.ds(c, blocks, stride=2), :] for c in range(2)], 1)
    s = spectrum(dot(fore_ref[:, :blocks], x.astype(BF16)))

    sr, si, fr, fi = s[:, :tok], s[:, tok:], f[:, :tok], f[:, tok:]
    y = jnp.concatenate([sr * fr - si * fi, sr * fi + si * fr], 1)
    g = dot(y.astype(BF16), qb_ref[...])
    parts = []
    for c in range(2):
        re, im = g[c * blocks : (c + 1) * blocks, :tok], g[c * blocks : (c + 1) * blocks, tok:]
        parts.append(jnp.concatenate([re * cos - im * sin, re * sin + im * cos], 0))
    out = dot(back_ref[...], jnp.concatenate(parts, 1).astype(BF16))
    for c in range(2):
        buf[pl.ds(c, blocks, stride=2), :] = out[:, c * tok : (c + 1) * tok]
    out_ref[...] = buf[...].astype(BF16)


def last_kernel(conv_ref, second_ref, direct_ref, w_ref, out_ref):
    gated = (second_ref[...] * (conv_ref[...].astype(F32) + direct_ref[...])).astype(BF16)
    out_ref[...] = lax.dot_general(
        gated, w_ref[...], (((0,), (0,)), ((), ())), preferred_element_type=F32
    ).astype(BF16)


def call(kernel, outs, scratch=()):
    many = isinstance(outs, (list, tuple))
    return pl.pallas_call(
        kernel,
        out_shape=outs,
        scratch_shapes=list(scratch),
        compiler_params=pltpu.CompilerParams(vmem_limit_bytes=40 * 1024 * 1024),
    )


def exchange(x):
    return lax.all_to_all(x, AXES, split_axis=0, concat_axis=0, tiled=True)


def body(tokens, w_in, conv_taps, causal_taps, anticausal_taps, skip_gain, w_out):
    rows = tokens.shape[0]
    channels, width = w_out.shape
    count = lax.axis_size(AXES)
    shape = jax.ShapeDtypeStruct
    vmem = pltpu.VMEM

    filt = call(
        filter_kernel,
        shape((2 * channels, rows), BF16),
        [vmem((channels, rows), F32), vmem((2 * channels, rows), F32)],
    )(causal_taps, anticausal_taps)
    filt = exchange(filt)

    before = lax.ppermute(tokens[-1:], AXES, [(i, i + 1) for i in range(count - 1)])
    after = lax.ppermute(tokens[:1], AXES, [(i + 1, i) for i in range(count - 1)])
    proj = dot(tokens, w_in).astype(BF16)
    edge = dot(jnp.concatenate([before, after], 0), w_in).astype(BF16)
    sig, second, direct = call(
        front_kernel,
        [shape((channels, rows), BF16), shape((channels, rows), F32), shape((channels, rows), F32)],
    )(proj, edge, conv_taps, skip_gain[None])
    sig = exchange(sig)

    conv = call(
        conv_kernel,
        shape((channels, rows), BF16),
        [vmem((channels, rows), F32), vmem((2 * channels, rows), F32)],
    )(sig, filt, *tables(count, rows))
    conv = exchange(conv)
    return call(last_kernel, shape((rows, width), BF16))(conv, second, direct, w_out)


def solution(mesh):
    rows = P(AXES, None)
    in_specs = (rows, P(), P(), rows, rows, P(), P())
    return jax.shard_map(body, mesh=mesh, in_specs=in_specs, out_specs=rows, check_vma=False)
```

```python
import math

import jax
import jax.numpy as jnp
import numpy as np
from jax import lax
from jax.experimental import pallas as pl
from jax.experimental.pallas import tpu as pltpu
from jax.sharding import PartitionSpec as P

AXES = ("blk", "fft")
F32 = jnp.float32
BF16 = jnp.bfloat16


def tables(blocks, tok):
    length = 2 * blocks * tok
    half = np.arange(blocks) + 0.5
    ang = 2 * math.pi * np.outer(half, np.arange(2 * blocks)) / (2 * blocks)
    fore = np.concatenate([np.cos(ang), -np.sin(ang)], 0)
    back = np.concatenate([fore[:blocks, :blocks].T, fore[blocks:, :blocks].T], 0) * (2 / length)
    fore[:, blocks:] *= -1
    twist = 2 * math.pi * np.outer(half, np.arange(tok)) / length
    inner = 2 * math.pi * np.outer(np.arange(tok), np.arange(tok)) / tok
    c, s = np.cos(inner), np.sin(inner)
    inner = np.block([[c, -s], [s, c], [c, s], [-s, c]])
    return (
        jnp.asarray(np.concatenate([fore, inner, back], 1), BF16),
        jnp.asarray(np.concatenate([np.cos(twist), np.sin(twist)], 1), F32),
    )


def dot(a, b):
    return jnp.dot(a, b, preferred_element_type=F32)


def front_kernel(
    tok_ref, before_ref, after_ref, w_ref, taps_ref, skip_ref, causal_ref, anti_ref, table_ref, twist_ref,
    send_ref, second_ref, direct_ref, table_out, twist_out, buf, wide, sems,
):
    copies = [
        pltpu.make_async_copy(table_ref, table_out, sems.at[0]),
        pltpu.make_async_copy(twist_ref, twist_out, sems.at[1]),
    ]
    for copy in copies:
        copy.start()
    rows = tok_ref.shape[0]
    channels = causal_ref.shape[1]
    half = channels // 2
    row = lax.broadcasted_iota(jnp.int32, (rows, channels), 0)
    tok = jnp.concatenate([tok_ref[...], before_ref[...], after_ref[...]], 0)

    def short(i):
        cols = slice(i * channels, (i + 1) * channels)
        proj = dot(tok, w_ref[:, cols]).astype(BF16).astype(F32)
        mid = proj[:rows]
        up = jnp.where(row == 0, proj[rows + 7 : rows + 8], pltpu.roll(mid, 1, 0))
        down = jnp.where(row == rows - 1, proj[rows + 8 : rows + 9], pltpu.roll(mid, rows - 1, 0))
        return taps_ref[0:1, cols] * up + taps_ref[1:2, cols] * mid + taps_ref[2:3, cols] * down

    def place(a, block):
        buf[...] = block.T
        for c in range(2):
            wide[pl.ds(2 * a + c, half, stride=6), :] = buf[pl.ds(c, half, stride=2), :]

    place(1, causal_ref[...].astype(F32))
    place(2, anti_ref[...].astype(F32))
    signal = short(0) * short(2)
    place(0, signal)
    send_ref[...] = wide[...].astype(BF16)
    second_ref[...] = short(1).T
    direct_ref[...] = (skip_ref[...] * signal).T
    for copy in copies:
        copy.wait()


def conv_kernel(got_ref, table_ref, twist_ref, out_ref, buf, wide):
    tok = got_ref.shape[1]
    blocks = got_ref.shape[0] // 6
    cos, sin = twist_ref[:, :tok], twist_ref[:, tok:]
    inner = slice(2 * blocks, 2 * blocks + 2 * tok)
    back = slice(2 * blocks + 2 * tok, 3 * blocks + 2 * tok)

    def spectrum(b):
        parts = []
        for c in range(2):
            lanes = slice(c * tok, (c + 1) * tok)
            re, im = b[:blocks, lanes], b[blocks:, lanes]
            parts.append(jnp.concatenate([re * cos + im * sin, im * cos - re * sin], 1))
        return dot(jnp.concatenate(parts, 0).astype(BF16), table_ref[: 2 * tok, inner])

    wide[...] = got_ref[...].astype(F32)
    sig, causal, anti = [
        jnp.concatenate([wide[pl.ds(2 * a + c, blocks, stride=6), :] for c in range(2)], 1)
        for a in range(3)
    ]
    place = lax.broadcasted_iota(jnp.int32, (blocks, 2 * tok), 0)
    lane = lax.broadcasted_iota(jnp.int32, (blocks, 2 * tok), 1)
    anti = jnp.where((place == 0) & (lane % tok == 0), 0.0, anti)
    f = spectrum(dot(table_ref[:, : 2 * blocks], jnp.concatenate([causal, anti], 0).astype(BF16)))
    s = spectrum(dot(table_ref[:, :blocks], sig.astype(BF16)))

    sr, si, fr, fi = s[:, :tok], s[:, tok:], f[:, :tok], f[:, tok:]
    y = jnp.concatenate([sr * fr - si * fi, sr * fi + si * fr], 1)
    g = dot(y.astype(BF16), table_ref[2 * tok : 4 * tok, inner])
    real, imag = [], []
    for c in range(2):
        re, im = g[c * blocks : (c + 1) * blocks, :tok], g[c * blocks : (c + 1) * blocks, tok:]
        real.append(re * cos - im * sin)
        imag.append(re * sin + im * cos)
    out = dot(table_ref[:blocks, back], jnp.concatenate(real, 1).astype(BF16))
    out += dot(table_ref[blocks : 2 * blocks, back], jnp.concatenate(imag, 1).astype(BF16))
    for c in range(2):
        buf[pl.ds(c, blocks, stride=2), :] = out[:, c * tok : (c + 1) * tok]
    out_ref[...] = buf[...].astype(BF16)


def last_kernel(conv_ref, second_ref, direct_ref, w_ref, out_ref):
    gated = (second_ref[...] * (conv_ref[...].astype(F32) + direct_ref[...])).astype(BF16)
    out_ref[...] = lax.dot_general(
        gated, w_ref[...], (((0,), (0,)), ((), ())), preferred_element_type=F32
    ).astype(BF16)


def call(kernel, outs, scratch=(), **specs):
    return pl.pallas_call(
        kernel,
        out_shape=outs,
        scratch_shapes=list(scratch),
        compiler_params=pltpu.CompilerParams(vmem_limit_bytes=24 * 1024 * 1024),
        **specs,
    )


def exchange(x):
    return lax.all_to_all(x, AXES, split_axis=0, concat_axis=0, tiled=True)


def body(tokens, w_in, conv_taps, causal_taps, anticausal_taps, skip_gain, w_out):
    rows = tokens.shape[0]
    channels, width = w_out.shape
    count = lax.axis_size(AXES)
    shape = jax.ShapeDtypeStruct
    vmem = pltpu.VMEM
    table, twist = tables(count, rows)

    before = lax.ppermute(tokens[-8:], AXES, [(i, i + 1) for i in range(count - 1)])
    after = lax.ppermute(tokens[:8], AXES, [(i + 1, i) for i in range(count - 1)])
    in_vmem, hbm = pl.BlockSpec(memory_space=vmem), pl.BlockSpec(memory_space=pltpu.HBM)
    send, second, direct, table, twist = call(
        front_kernel,
        [
            shape((3 * channels, rows), BF16),
            shape((channels, rows), F32),
            shape((channels, rows), F32),
            shape(table.shape, table.dtype),
            shape(twist.shape, twist.dtype),
        ],
        [vmem((channels, rows), F32), vmem((3 * channels, rows), F32), pltpu.SemaphoreType.DMA((2,))],
        in_specs=[in_vmem] * 8 + [hbm] * 2,
        out_specs=[in_vmem] * 5,
    )(tokens, before, after, w_in, conv_taps, skip_gain[None], causal_taps, anticausal_taps, table, twist)
    got = exchange(send.reshape(-1, 2, rows)).reshape(send.shape)

    conv = call(
        conv_kernel,
        shape((channels, rows), BF16),
        [vmem((channels, rows), F32), vmem((3 * channels, rows), F32)],
    )(got, table, twist)
    conv = exchange(conv)
    return call(last_kernel, shape((rows, width), BF16))(conv, second, direct, w_out)


def solution(mesh):
    rows = P(AXES, None)
    in_specs = (rows, P(), P(), rows, rows, P(), P())
    return jax.shard_map(body, mesh=mesh, in_specs=in_specs, out_specs=rows, check_vma=False)
```

```python
import math

import jax
import jax.numpy as jnp
import numpy as np
from jax import lax
from jax.experimental import pallas as pl
from jax.experimental.pallas import tpu as pltpu
from jax.sharding import PartitionSpec as P

AXES = ("blk", "fft")
F32 = jnp.float32
BF16 = jnp.bfloat16


def tables(blocks, tok):
    length = 2 * blocks * tok
    half = np.arange(blocks) + 0.5
    ang = 2 * math.pi * np.outer(half, np.arange(2 * blocks)) / (2 * blocks)
    fore = np.concatenate([np.cos(ang), -np.sin(ang)], 0)
    back = np.concatenate([fore[:blocks, :blocks].T, fore[blocks:, :blocks].T], 0) * (2 / length)
    fore[:, blocks:] *= -1
    twist = 2 * math.pi * np.outer(half, np.arange(tok)) / length
    inner = 2 * math.pi * np.outer(np.arange(tok), np.arange(tok)) / tok
    c, s = np.cos(inner), np.sin(inner)
    inner = np.block([[c, -s], [s, c], [c, s], [-s, c]])
    return (
        jnp.asarray(np.concatenate([fore, inner, back], 1), BF16),
        jnp.asarray(np.concatenate([np.cos(twist), np.sin(twist)], 1), F32),
    )


def dot(a, b):
    return jnp.dot(a, b, preferred_element_type=F32)


def front_kernel(
    tok_hbm, w_hbm, taps_hbm, skip_hbm, causal_hbm, anti_hbm,
    send_ref, second_ref, direct_ref,
    tok_ref, w_ref, taps_ref, skip_ref, causal_ref, anti_ref, buf, wide, sems,
):
    rows = tok_ref.shape[0]
    channels = causal_ref.shape[1]
    half = channels // 2

    def slab(i):
        return slice(i * channels, (i + 1) * channels)

    pairs = [(causal_hbm, causal_ref), (anti_hbm, anti_ref), (tok_hbm, tok_ref)]
    pairs += [(w_hbm.at[:, slab(i)], w_ref.at[:, slab(i)]) for i in (0, 2, 1)]
    pairs += [(taps_hbm, taps_ref), (skip_hbm, skip_ref)]
    copies = [pltpu.make_async_copy(a, b, sems.at[i]) for i, (a, b) in enumerate(pairs)]
    for copy in copies:
        copy.start()

    def place(a, block):
        buf[...] = block.T
        for c in range(2):
            wide[pl.ds(2 * a + c, half, stride=8), :] = buf[pl.ds(c, half, stride=2), :]

    copies[0].wait()
    place(1, causal_ref[...].astype(F32))
    copies[1].wait()
    place(2, anti_ref[...].astype(F32))
    copies[6].wait()
    copies[7].wait()
    copies[2].wait()
    row = lax.broadcasted_iota(jnp.int32, (rows, channels), 0)

    def short(i, copy):
        copy.wait()
        proj = dot(tok_ref[...], w_ref[:, slab(i)]).astype(BF16).astype(F32)
        prior, here, after = [taps_ref[k : k + 1, slab(i)] for k in range(3)]
        up = jnp.where(row == 0, 0.0, pltpu.roll(proj, 1, 0))
        down = jnp.where(row == rows - 1, 0.0, pltpu.roll(proj, rows - 1, 0))
        return prior * up + here * proj + after * down, after * proj[:1], prior * proj[rows - 1 :]

    first, first_up, first_down = short(0, copies[3])
    value, value_up, value_down = short(2, copies[4])
    signal = first * value
    place(0, signal)
    direct_ref[...] = (skip_ref[...] * signal).T
    second, second_up, second_down = short(1, copies[5])
    second_ref[...] = second.T
    last = rows - 1
    ends = [
        first[:1], value[last:], value[:1], second[last:], second[:1],
        first_up, first_down, value_up, value_down, second_up, second_down,
        skip_ref[...], skip_ref[...],
    ]
    fill = jnp.zeros((rows - len(ends) - 1, channels), F32)
    place(3, jnp.concatenate(ends + [fill, first[last:]], 0))
    send_ref[...] = wide[...].astype(BF16)


def conv_kernel(got_ref, table_ref, twist_ref, out_ref, buf, wide):
    tok = got_ref.shape[1]
    blocks = got_ref.shape[0] // 8
    cos, sin = twist_ref[:, :tok], twist_ref[:, tok:]
    inner = slice(2 * blocks, 2 * blocks + 2 * tok)
    back = slice(2 * blocks + 2 * tok, 3 * blocks + 2 * tok)
    place = lax.broadcasted_iota(jnp.int32, (blocks, tok), 0)
    lane = lax.broadcasted_iota(jnp.int32, (blocks, tok), 1)
    at_end = (lane == 0) | (lane == tok - 1)

    def left(x, n):
        return pltpu.roll(x, tok - n, 1)

    def take(a, c):
        return wide[pl.ds(2 * a + c, blocks, stride=8), :]

    def spectrum(b):
        parts = []
        for c in range(2):
            lanes = slice(c * tok, (c + 1) * tok)
            re, im = b[:blocks, lanes], b[blocks:, lanes]
            parts.append(jnp.concatenate([re * cos + im * sin, im * cos - re * sin], 1))
        return dot(jnp.concatenate(parts, 0).astype(BF16), table_ref[: 2 * tok, inner])

    wide[...] = got_ref[...].astype(F32)
    causal = jnp.concatenate([take(1, 0), take(1, 1)], 1)
    anti = jnp.concatenate(
        [jnp.where((place == 0) & (lane == 0), 0.0, take(2, c)) for c in range(2)], 1
    )
    f = spectrum(dot(table_ref[:, : 2 * blocks], jnp.concatenate([causal, anti], 0).astype(BF16)))

    signal, end_signal, end_second, end_skip = [], [], [], []
    for c in range(2):
        ends = take(3, c)
        prior = jnp.where(place == 0, 0.0, pltpu.roll(ends, 1, 0))
        after = jnp.where(place == blocks - 1, 0.0, pltpu.roll(ends, blocks - 1, 0))
        full = ends + left(jnp.where(lane % 2 == 1, after, prior), 6)
        end_signal.append(full * left(full, 2))
        end_second.append(left(full, 4))
        end_skip.append(left(ends, 12))
        signal.append(jnp.where(at_end, end_signal[c], take(0, c)))
    s = spectrum(dot(table_ref[:, :blocks], jnp.concatenate(signal, 1).astype(BF16)))

    sr, si, fr, fi = s[:, :tok], s[:, tok:], f[:, :tok], f[:, tok:]
    y = jnp.concatenate([sr * fr - si * fi, sr * fi + si * fr], 1)
    g = dot(y.astype(BF16), table_ref[2 * tok : 4 * tok, inner])
    real, imag = [], []
    for c in range(2):
        re, im = g[c * blocks : (c + 1) * blocks, :tok], g[c * blocks : (c + 1) * blocks, tok:]
        real.append(re * cos - im * sin)
        imag.append(re * sin + im * cos)
    out = dot(table_ref[:blocks, back], jnp.concatenate(real, 1).astype(BF16))
    out += dot(table_ref[blocks : 2 * blocks, back], jnp.concatenate(imag, 1).astype(BF16))
    for c in range(2):
        conv = out[:, c * tok : (c + 1) * tok]
        gated = end_second[c] * (conv + end_skip[c] * end_signal[c])
        buf[pl.ds(c, blocks, stride=2), :] = jnp.where(at_end, gated, conv)
    out_ref[...] = buf[...].astype(BF16)


def last_kernel(conv_ref, second_ref, direct_ref, w_ref, out_ref):
    conv = conv_ref[...].astype(F32)
    lane = lax.broadcasted_iota(jnp.int32, conv.shape, 1)
    at_end = (lane == 0) | (lane == conv.shape[1] - 1)
    gated = jnp.where(at_end, conv, second_ref[...] * (conv + direct_ref[...])).astype(BF16)
    out_ref[...] = lax.dot_general(
        gated, w_ref[...], (((0,), (0,)), ((), ())), preferred_element_type=F32
    ).astype(BF16)


def call(kernel, outs, scratch=(), mib=24, **specs):
    return pl.pallas_call(
        kernel,
        out_shape=outs,
        scratch_shapes=list(scratch),
        compiler_params=pltpu.CompilerParams(vmem_limit_bytes=mib * 1024 * 1024),
        **specs,
    )


def exchange(x):
    return lax.all_to_all(x, AXES, split_axis=0, concat_axis=0, tiled=True)


def body(tokens, w_in, conv_taps, causal_taps, anticausal_taps, skip_gain, w_out):
    rows = tokens.shape[0]
    channels, width = w_out.shape
    count = lax.axis_size(AXES)
    shape = jax.ShapeDtypeStruct
    vmem = pltpu.VMEM
    table, twist = tables(count, rows)

    hbm = pl.BlockSpec(memory_space=pltpu.HBM)
    staged = (tokens, w_in, conv_taps, skip_gain[None], causal_taps, anticausal_taps)
    send, second, direct = call(
        front_kernel,
        [shape((4 * channels, rows), BF16), shape((channels, rows), F32), shape((channels, rows), F32)],
        [vmem(x.shape, x.dtype) for x in staged]
        + [vmem((channels, rows), F32), vmem((4 * channels, rows), F32), pltpu.SemaphoreType.DMA((8,))],
        mib=60,
        in_specs=[hbm] * 6,
    )(*staged)
    got = exchange(send.reshape(count, 8, rows)).reshape(send.shape)

    conv = call(
        conv_kernel,
        shape((channels, rows), BF16),
        [vmem((channels, rows), F32), vmem((4 * channels, rows), F32)],
    )(got, table, twist)
    conv = exchange(conv)
    return call(last_kernel, shape((rows, width), BF16))(conv, second, direct, w_out)


def solution(mesh):
    rows = P(AXES, None)
    in_specs = (rows, P(), P(), rows, rows, P(), P())
    return jax.shard_map(body, mesh=mesh, in_specs=in_specs, out_specs=rows, check_vma=False)
```

```python
import math

import jax
import jax.numpy as jnp
import numpy as np
from jax import lax
from jax.experimental import pallas as pl
from jax.experimental.pallas import tpu as pltpu
from jax.sharding import PartitionSpec as P

AXES = ("blk", "fft")
F32 = jnp.float32
BF16 = jnp.bfloat16


def tables(blocks, tok):
    length = 2 * blocks * tok
    half = np.arange(blocks) + 0.5
    ang = 2 * math.pi * np.outer(half, np.arange(2 * blocks)) / (2 * blocks)
    fore = np.concatenate([np.cos(ang), -np.sin(ang)], 0)
    back = np.concatenate([fore[:blocks, :blocks].T, fore[blocks:, :blocks].T], 0) * (2 / length)
    fore[:, blocks:] *= -1
    twist = 2 * math.pi * np.outer(half, np.arange(tok)) / length
    inner = 2 * math.pi * np.outer(np.arange(tok), np.arange(tok)) / tok
    c, s = np.cos(inner), np.sin(inner)
    inner = np.block([[c, -s], [s, c], [c, s], [-s, c]])
    return (
        jnp.asarray(np.concatenate([fore, inner, back], 1), BF16),
        jnp.asarray(np.concatenate([np.cos(twist), np.sin(twist)], 1), F32),
    )


def dot(a, b):
    return jnp.dot(a, b, preferred_element_type=F32)


def first_kernel(out_ref):
    out_ref[...] = jnp.zeros_like(out_ref)


def front_kernel(
    start_ref, tok_ref, w_ref, taps_ref, skip_ref, causal_ref, anti_ref,
    send_ref, second_ref, direct_ref, buf, wide,
):
    rows = tok_ref.shape[0]
    channels = causal_ref.shape[1]
    half = channels // 2
    row = lax.broadcasted_iota(jnp.int32, (rows, channels), 0)

    def slab(i):
        return slice(i * channels, (i + 1) * channels)

    def place(a, block):
        buf[...] = block.T
        for c in range(2):
            wide[pl.ds(2 * a + c, half, stride=8), :] = buf[pl.ds(c, half, stride=2), :]

    def short(i):
        proj = dot(tok_ref[...], w_ref[:, slab(i)]).astype(BF16).astype(F32)
        prior, here, after = [taps_ref[k : k + 1, slab(i)] for k in range(3)]
        up = jnp.where(row == 0, 0.0, pltpu.roll(proj, 1, 0))
        down = jnp.where(row == rows - 1, 0.0, pltpu.roll(proj, rows - 1, 0))
        return prior * up + here * proj + after * down, after * proj[:1], prior * proj[rows - 1 :]

    place(1, causal_ref[...].astype(F32))
    place(2, anti_ref[...].astype(F32))
    first, first_up, first_down = short(0)
    value, value_up, value_down = short(2)
    signal = first * value
    place(0, signal)
    direct_ref[...] = (skip_ref[...] * signal).T
    second, second_up, second_down = short(1)
    second_ref[...] = second.T
    last = rows - 1
    ends = [
        first[:1], value[last:], value[:1], second[last:], second[:1],
        first_up, first_down, value_up, value_down, second_up, second_down,
        skip_ref[...], skip_ref[...],
    ]
    fill = jnp.zeros((rows - len(ends) - 1, channels), F32)
    place(3, jnp.concatenate(ends + [fill, first[last:]], 0))
    send_ref[...] = wide[...].astype(BF16)


def conv_kernel(got_ref, table_ref, twist_ref, out_ref, buf, wide):
    tok = got_ref.shape[1]
    blocks = got_ref.shape[0] // 8
    cos, sin = twist_ref[:, :tok], twist_ref[:, tok:]
    inner = slice(2 * blocks, 2 * blocks + 2 * tok)
    back = slice(2 * blocks + 2 * tok, 3 * blocks + 2 * tok)
    place = lax.broadcasted_iota(jnp.int32, (blocks, tok), 0)
    lane = lax.broadcasted_iota(jnp.int32, (blocks, tok), 1)
    at_end = (lane == 0) | (lane == tok - 1)

    def left(x, n):
        return pltpu.roll(x, tok - n, 1)

    def take(a, c):
        return wide[pl.ds(2 * a + c, blocks, stride=8), :]

    def spectrum(b):
        parts = []
        for c in range(2):
            lanes = slice(c * tok, (c + 1) * tok)
            re, im = b[:blocks, lanes], b[blocks:, lanes]
            parts.append(jnp.concatenate([re * cos + im * sin, im * cos - re * sin], 1))
        return dot(jnp.concatenate(parts, 0).astype(BF16), table_ref[: 2 * tok, inner])

    wide[...] = got_ref[...].astype(F32)
    causal = jnp.concatenate([take(1, 0), take(1, 1)], 1)
    anti = jnp.concatenate(
        [jnp.where((place == 0) & (lane == 0), 0.0, take(2, c)) for c in range(2)], 1
    )
    f = spectrum(dot(table_ref[:, : 2 * blocks], jnp.concatenate([causal, anti], 0).astype(BF16)))

    signal, end_signal, end_second, end_skip = [], [], [], []
    for c in range(2):
        ends = take(3, c)
        prior = jnp.where(place == 0, 0.0, pltpu.roll(ends, 1, 0))
        after = jnp.where(place == blocks - 1, 0.0, pltpu.roll(ends, blocks - 1, 0))
        full = ends + left(jnp.where(lane % 2 == 1, after, prior), 6)
        end_signal.append(full * left(full, 2))
        end_second.append(left(full, 4))
        end_skip.append(left(ends, 12))
        signal.append(jnp.where(at_end, end_signal[c], take(0, c)))
    s = spectrum(dot(table_ref[:, :blocks], jnp.concatenate(signal, 1).astype(BF16)))

    sr, si, fr, fi = s[:, :tok], s[:, tok:], f[:, :tok], f[:, tok:]
    y = jnp.concatenate([sr * fr - si * fi, sr * fi + si * fr], 1)
    g = dot(y.astype(BF16), table_ref[2 * tok : 4 * tok, inner])
    real, imag = [], []
    for c in range(2):
        re, im = g[c * blocks : (c + 1) * blocks, :tok], g[c * blocks : (c + 1) * blocks, tok:]
        real.append(re * cos - im * sin)
        imag.append(re * sin + im * cos)
    out = dot(table_ref[:blocks, back], jnp.concatenate(real, 1).astype(BF16))
    out += dot(table_ref[blocks : 2 * blocks, back], jnp.concatenate(imag, 1).astype(BF16))
    for c in range(2):
        conv = out[:, c * tok : (c + 1) * tok]
        gated = end_second[c] * (conv + end_skip[c] * end_signal[c])
        buf[pl.ds(c, blocks, stride=2), :] = jnp.where(at_end, gated, conv)
    out_ref[...] = buf[...].astype(BF16)


def last_kernel(conv_ref, second_ref, direct_ref, w_ref, out_ref):
    conv = conv_ref[...].astype(F32)
    lane = lax.broadcasted_iota(jnp.int32, conv.shape, 1)
    at_end = (lane == 0) | (lane == conv.shape[1] - 1)
    gated = jnp.where(at_end, conv, second_ref[...] * (conv + direct_ref[...])).astype(BF16)
    out_ref[...] = lax.dot_general(
        gated, w_ref[...], (((0,), (0,)), ((), ())), preferred_element_type=F32
    ).astype(BF16)


def call(kernel, outs, scratch=(), mib=24, cost=0, **specs):
    return pl.pallas_call(
        kernel,
        out_shape=outs,
        scratch_shapes=list(scratch),
        compiler_params=pltpu.CompilerParams(vmem_limit_bytes=mib * 1024 * 1024),
        cost_estimate=pl.CostEstimate(flops=cost, bytes_accessed=0, transcendentals=0) if cost else None,
        **specs,
    )


def exchange(x):
    return lax.all_to_all(x, AXES, split_axis=0, concat_axis=0, tiled=True)


def body(tokens, w_in, conv_taps, causal_taps, anticausal_taps, skip_gain, w_out):
    rows = tokens.shape[0]
    channels, width = w_out.shape
    count = lax.axis_size(AXES)
    shape = jax.ShapeDtypeStruct
    vmem = pltpu.VMEM
    table, twist = tables(count, rows)

    staged = (tokens, w_in, conv_taps, skip_gain[None], causal_taps, anticausal_taps)
    start = call(first_kernel, shape((8, 128), F32), cost=20000000000)()
    send, second, direct = call(
        front_kernel,
        [shape((4 * channels, rows), BF16), shape((channels, rows), F32), shape((channels, rows), F32)],
        [vmem((channels, rows), F32), vmem((4 * channels, rows), F32)],
    )(start, *staged)
    got = exchange(send.reshape(count, 8, rows)).reshape(send.shape)

    conv = call(
        conv_kernel,
        shape((channels, rows), BF16),
        [vmem((channels, rows), F32), vmem((4 * channels, rows), F32)],
    )(got, table, twist)
    conv = exchange(conv)
    return call(last_kernel, shape((rows, width), BF16))(conv, second, direct, w_out)


def solution(mesh):
    rows = P(AXES, None)
    in_specs = (rows, P(), P(), rows, rows, P(), P())
    return jax.shard_map(body, mesh=mesh, in_specs=in_specs, out_specs=rows, check_vma=False)
```

```python
import math

import jax
import jax.numpy as jnp
import numpy as np
from jax import lax
from jax.experimental import pallas as pl
from jax.experimental.pallas import tpu as pltpu
from jax.sharding import PartitionSpec as P

AXES = ("blk", "fft")
F32 = jnp.float32
BF16 = jnp.bfloat16


def tables(blocks, tok):
    length = 2 * blocks * tok
    half = np.arange(blocks) + 0.5
    ang = 2 * math.pi * np.outer(half, np.arange(2 * blocks)) / (2 * blocks)
    fore = np.concatenate([np.cos(ang), -np.sin(ang)], 0)
    back = np.concatenate([fore[:blocks, :blocks].T, fore[blocks:, :blocks].T], 0) * (2 / length)
    fore[:, blocks:] *= -1
    inner = 2 * math.pi * np.outer(np.arange(tok), np.arange(tok)) / tok
    c, s = np.cos(inner), np.sin(inner)
    inner = np.block([[c, -s], [s, c], [c, s], [-s, c]])
    return jnp.asarray(np.concatenate([fore, inner, back], 1), BF16)


def dot(a, b):
    return jnp.dot(a, b, preferred_element_type=F32)


def first_kernel(twist_ref):
    blocks, tok = twist_ref.shape[0], twist_ref.shape[1] // 2
    k = lax.broadcasted_iota(jnp.int32, (blocks, tok), 0)
    t = lax.broadcasted_iota(jnp.int32, (blocks, tok), 1)
    angle = ((2 * k + 1) * t).astype(F32) * (math.pi / (2 * blocks * tok))
    twist_ref[:, :tok] = jnp.cos(angle)
    twist_ref[:, tok:] = jnp.sin(angle)


def front_kernel(
    _, tok_ref, w_ref, taps_ref, skip_ref, causal_ref, anti_ref,
    send_ref, second_ref, direct_ref, buf, wide,
):
    rows = tok_ref.shape[0]
    channels = causal_ref.shape[1]
    half = channels // 2
    row = lax.broadcasted_iota(jnp.int32, (rows, channels), 0)

    def slab(i):
        return slice(i * channels, (i + 1) * channels)

    def place(a, block):
        buf[...] = block.T
        for c in range(2):
            wide[pl.ds(2 * a + c, half, stride=8), :] = buf[pl.ds(c, half, stride=2), :]

    def short(i):
        proj = dot(tok_ref[...], w_ref[:, slab(i)]).astype(BF16).astype(F32)
        prior, here, after = [taps_ref[k : k + 1, slab(i)] for k in range(3)]
        up = jnp.where(row == 0, 0.0, pltpu.roll(proj, 1, 0))
        down = jnp.where(row == rows - 1, 0.0, pltpu.roll(proj, rows - 1, 0))
        return prior * up + here * proj + after * down, after * proj[:1], prior * proj[rows - 1 :]

    place(1, causal_ref[...].astype(F32))
    place(2, anti_ref[...].astype(F32))
    first, first_up, first_down = short(0)
    value, value_up, value_down = short(2)
    signal = first * value
    place(0, signal)
    direct_ref[...] = (skip_ref[...] * signal).T
    second, second_up, second_down = short(1)
    second_ref[...] = second.T
    last = rows - 1
    ends = [
        first[:1], value[last:], value[:1], second[last:], second[:1],
        first_up, first_down, value_up, value_down, second_up, second_down,
        skip_ref[...], skip_ref[...],
    ]
    fill = jnp.zeros((rows - len(ends) - 1, channels), F32)
    place(3, jnp.concatenate(ends + [fill, first[last:]], 0))
    send_ref[...] = wide[...].astype(BF16)


def conv_kernel(got_ref, table_ref, twist_ref, out_ref, buf, wide):
    tok = got_ref.shape[1]
    blocks = got_ref.shape[0] // 8
    cos, sin = twist_ref[:, :tok], twist_ref[:, tok:]
    inner = slice(2 * blocks, 2 * blocks + 2 * tok)
    back = slice(2 * blocks + 2 * tok, 3 * blocks + 2 * tok)
    place = lax.broadcasted_iota(jnp.int32, (blocks, tok), 0)
    lane = lax.broadcasted_iota(jnp.int32, (blocks, tok), 1)
    at_end = (lane == 0) | (lane == tok - 1)

    def left(x, n):
        return pltpu.roll(x, tok - n, 1)

    def take(a, c):
        return wide[pl.ds(2 * a + c, blocks, stride=8), :]

    def spectrum(b):
        parts = []
        for c in range(2):
            lanes = slice(c * tok, (c + 1) * tok)
            re, im = b[:blocks, lanes], b[blocks:, lanes]
            parts.append(jnp.concatenate([re * cos + im * sin, im * cos - re * sin], 1))
        return [dot(part.astype(BF16), table_ref[: 2 * tok, inner]) for part in parts]

    wide[...] = got_ref[...].astype(F32)
    causal = jnp.concatenate([take(1, 0), take(1, 1)], 1)
    anti = jnp.concatenate(
        [jnp.where((place == 0) & (lane == 0), 0.0, take(2, c)) for c in range(2)], 1
    )
    f = spectrum(dot(table_ref[:, : 2 * blocks], jnp.concatenate([causal, anti], 0).astype(BF16)))

    signal, end_signal, end_second, end_skip = [], [], [], []
    for c in range(2):
        ends = take(3, c)
        prior = jnp.where(place == 0, 0.0, pltpu.roll(ends, 1, 0))
        after = jnp.where(place == blocks - 1, 0.0, pltpu.roll(ends, blocks - 1, 0))
        full = ends + left(jnp.where(lane % 2 == 1, after, prior), 6)
        end_signal.append(full * left(full, 2))
        end_second.append(left(full, 4))
        end_skip.append(left(ends, 12))
        signal.append(jnp.where(at_end, end_signal[c], take(0, c)))
    s = spectrum(dot(table_ref[:, :blocks], jnp.concatenate(signal, 1).astype(BF16)))

    real, imag = [], []
    for c in range(2):
        sr, si, fr, fi = s[c][:, :tok], s[c][:, tok:], f[c][:, :tok], f[c][:, tok:]
        y = jnp.concatenate([sr * fr - si * fi, sr * fi + si * fr], 1)
        g = dot(y.astype(BF16), table_ref[2 * tok : 4 * tok, inner])
        re, im = g[:, :tok], g[:, tok:]
        real.append(re * cos - im * sin)
        imag.append(re * sin + im * cos)
    e = jnp.concatenate([jnp.concatenate(real, 1), jnp.concatenate(imag, 1)], 0)
    out = dot(jnp.concatenate([table_ref[:blocks, back], table_ref[blocks : 2 * blocks, back]], 1), e.astype(BF16))
    for c in range(2):
        conv = out[:, c * tok : (c + 1) * tok]
        gated = end_second[c] * (conv + end_skip[c] * end_signal[c])
        buf[pl.ds(c, blocks, stride=2), :] = jnp.where(at_end, gated, conv)
    out_ref[...] = buf[...].astype(BF16)


def last_kernel(conv_ref, second_ref, direct_ref, w_ref, out_ref):
    conv = conv_ref[...].astype(F32)
    lane = lax.broadcasted_iota(jnp.int32, conv.shape, 1)
    at_end = (lane == 0) | (lane == conv.shape[1] - 1)
    gated = jnp.where(at_end, conv, second_ref[...] * (conv + direct_ref[...])).astype(BF16)
    out_ref[...] = lax.dot_general(
        gated, w_ref[...], (((0,), (0,)), ((), ())), preferred_element_type=F32
    ).astype(BF16)


def call(kernel, outs, scratch=(), mib=24, cost=0, **specs):
    return pl.pallas_call(
        kernel,
        out_shape=outs,
        scratch_shapes=list(scratch),
        compiler_params=pltpu.CompilerParams(vmem_limit_bytes=mib * 1024 * 1024),
        cost_estimate=pl.CostEstimate(flops=cost, bytes_accessed=0, transcendentals=0) if cost else None,
        **specs,
    )


def exchange(x):
    return lax.all_to_all(x, AXES, split_axis=0, concat_axis=0, tiled=True)


def body(tokens, w_in, conv_taps, causal_taps, anticausal_taps, skip_gain, w_out):
    rows = tokens.shape[0]
    channels, width = w_out.shape
    count = lax.axis_size(AXES)
    shape = jax.ShapeDtypeStruct
    vmem = pltpu.VMEM
    table = tables(count, rows)

    staged = (tokens, w_in, conv_taps, skip_gain[None], causal_taps, anticausal_taps)
    twist = call(first_kernel, shape((count, 2 * rows), F32), cost=2 * 10**9)()
    send, second, direct = call(
        front_kernel,
        [shape((4 * channels, rows), BF16), shape((channels, rows), F32), shape((channels, rows), F32)],
        [vmem((channels, rows), F32), vmem((4 * channels, rows), F32)],
    )(twist, *staged)
    got = exchange(send.reshape(count, 8, rows)).reshape(send.shape)

    conv = call(
        conv_kernel,
        shape((channels, rows), BF16),
        [vmem((channels, rows), F32), vmem((4 * channels, rows), F32)],
    )(got, table, twist)
    conv = exchange(conv)
    return call(last_kernel, shape((rows, width), BF16))(conv, second, direct, w_out)


def solution(mesh):
    rows = P(AXES, None)
    in_specs = (rows, P(), P(), rows, rows, P(), P())
    return jax.shard_map(body, mesh=mesh, in_specs=in_specs, out_specs=rows, check_vma=False)
```

```python
import math

import jax
import jax.numpy as jnp
import numpy as np
from jax import lax
from jax.experimental import pallas as pl
from jax.experimental.pallas import tpu as pltpu
from jax.sharding import PartitionSpec as P

AXES = ("blk", "fft")
F32 = jnp.float32
BF16 = jnp.bfloat16


def tables(blocks, tok):
    length = 2 * blocks * tok
    half = np.arange(blocks) + 0.5
    ang = 2 * math.pi * np.outer(half, np.arange(2 * blocks)) / (2 * blocks)
    fore = np.concatenate([np.cos(ang), -np.sin(ang)], 0)
    back = np.concatenate([fore[:blocks, :blocks].T, fore[blocks:, :blocks].T], 0) * (2 / length)
    fore[:, blocks:] *= -1
    order = np.arange(blocks).reshape(-1, 2).T.reshape(-1)
    fore = fore[:, np.concatenate([order, order + blocks])]
    back = np.concatenate([back[:blocks][order], back[blocks:][order]], 0)
    inner = 2 * math.pi * np.outer(np.arange(tok), np.arange(tok)) / tok
    c, s = np.cos(inner), np.sin(inner)
    inner = np.block([[c, -s], [s, c], [c, s], [-s, c]])
    return jnp.asarray(np.concatenate([fore, inner, back], 1), BF16)


def dot(a, b):
    return jnp.dot(a, b, preferred_element_type=F32)


def first_kernel(twist_ref):
    blocks, tok = twist_ref.shape[0], twist_ref.shape[1] // 2
    k = lax.broadcasted_iota(jnp.int32, (blocks, tok), 0)
    t = lax.broadcasted_iota(jnp.int32, (blocks, tok), 1)
    angle = ((2 * k + 1) * t).astype(F32) * (math.pi / (2 * blocks * tok))
    twist_ref[:, :tok] = jnp.cos(angle)
    twist_ref[:, tok:] = jnp.sin(angle)


def front_kernel(
    _, tok_ref, tok_mate_ref, w_ref, taps_ref, causal_ref, causal_mate_ref, anti_ref, anti_mate_ref,
    send_ref, second_ref, tok, ends_ref, buf, wide,
):
    rows = tok_ref.shape[0]
    channels = causal_ref.shape[1]
    half = channels // 2
    chips = wide.shape[0] // 14
    core = lax.axis_index("fft") % 2
    last = 2 * rows - 1

    def mine(i):
        return pl.ds(pl.multiple_of(i * channels + core * half, half), half)

    def place(at, block):
        buf[...] = block.T
        for c in range(2):
            wide[pl.ds(at + c, chips, stride=14), :] = buf[pl.ds(c, chips, stride=2), :]

    own_rows = pl.ds(pl.multiple_of(core * rows, rows), rows)
    tok[own_rows, :] = tok_ref[...]
    tok[pl.ds(pl.multiple_of((1 - core) * rows, rows), rows), :] = tok_mate_ref[...]

    for a, (ref, mate_ref) in enumerate(((causal_ref, causal_mate_ref), (anti_ref, anti_mate_ref))):
        own, mate = ref[:, mine(0)].astype(F32), mate_ref[:, mine(0)].astype(F32)
        place(4 * a + 4, jnp.where(core == 0, own, mate))
        place(4 * a + 6, jnp.where(core == 0, mate, own))

    def short(i, cols):
        proj = dot(tok[...], w_ref[:, cols]).astype(BF16).astype(F32)
        row = lax.broadcasted_iota(jnp.int32, proj.shape, 0)
        prior, here, after = [taps_ref[k : k + 1, cols] for k in range(3)]
        up = jnp.where(row == 0, 0.0, pltpu.roll(proj, 1, 0))
        down = jnp.where(row == last, 0.0, pltpu.roll(proj, last, 0))
        return prior * up + here * proj + after * down, after * proj[:1], prior * proj[last:]

    first, first_up, first_down = short(0, mine(0))
    value, value_up, value_down = short(2, mine(2))
    signal = first * value
    place(0, signal[:rows])
    place(2, signal[rows:])
    cols = slice(channels, 2 * channels)
    near = jnp.concatenate([tok_ref[...], tok_mate_ref[:8], tok_mate_ref[rows - 8 :]], 0)
    proj = dot(near, w_ref[:, cols]).astype(BF16).astype(F32)
    own, mate = proj[:rows], proj[rows:]
    row = lax.broadcasted_iota(jnp.int32, own.shape, 0)
    prior, here, after = [taps_ref[k : k + 1, cols] for k in range(3)]
    up = jnp.where(row == 0, jnp.where(core == 0, 0.0, mate[15:]), pltpu.roll(own, 1, 0))
    down = jnp.where(row == rows - 1, jnp.where(core == 0, mate[:1], 0.0), pltpu.roll(own, rows - 1, 0))
    second = prior * up + here * own + after * down
    second_ref[...] = second.T
    ends_ref[...] = jnp.concatenate(
        [
            jnp.where(core == 0, prior * mate[14:15] + here * mate[15:], second[rows - 1 :]),
            jnp.where(core == 0, second[:1], here * mate[:1] + after * mate[1:2]),
            after * jnp.where(core == 0, own[:1], mate[:1]),
            prior * jnp.where(core == 0, mate[15:], own[rows - 1 :]),
            jnp.zeros((4, channels), F32),
        ],
        0,
    )
    part = ends_ref[:, mine(0)]
    ends = [
        first[:1], value[last:], value[:1], part[:1], part[1:2],
        first_up, first_down, value_up, value_down, part[2:3], part[3:4],
    ]
    fill = jnp.zeros((rows - len(ends) - 1, half), F32)
    place(12, jnp.concatenate(ends + [fill, first[last:]], 0))
    send_ref[...] = wide[...].astype(BF16)


def conv_kernel(got_ref, skip_ref, table_ref, twist_ref, out_ref, buf, wide):
    tok = got_ref.shape[1]
    chips = got_ref.shape[0] // 14
    blocks = 2 * chips
    cos, sin = twist_ref[:, :tok], twist_ref[:, tok:]
    inner = slice(2 * blocks, 2 * blocks + 2 * tok)
    back = slice(2 * blocks + 2 * tok, 3 * blocks + 2 * tok)
    place = lax.broadcasted_iota(jnp.int32, (chips, tok), 0)
    lane = lax.broadcasted_iota(jnp.int32, (chips, tok), 1)
    fft = lax.axis_index("fft")
    owner = fft % 2 * blocks + 2 * (lax.axis_index("blk") * (lax.axis_size("fft") // 2) + fft // 2)

    def left(x, n):
        return pltpu.roll(x, tok - n, 1)

    def take(at):
        return wide[pl.ds(at, chips, stride=14), :]

    def taps(a):
        return jnp.concatenate(
            [jnp.concatenate([take(a + 2 * h + c) for c in range(2)], 1) for h in range(2)], 0
        )

    def spectrum(b):
        parts = []
        for c in range(2):
            lanes = slice(c * tok, (c + 1) * tok)
            re, im = b[:blocks, lanes], b[blocks:, lanes]
            parts.append(jnp.concatenate([re * cos + im * sin, im * cos - re * sin], 1))
        return [dot(part.astype(BF16), table_ref[: 2 * tok, inner]) for part in parts]

    wide[...] = got_ref[...].astype(F32)
    anti = taps(8)
    row = lax.broadcasted_iota(jnp.int32, anti.shape, 0)
    col = lax.broadcasted_iota(jnp.int32, anti.shape, 1)
    anti = jnp.where((row == 0) & (col % tok == 0), 0.0, anti)
    f = spectrum(dot(table_ref[:, : 2 * blocks], jnp.concatenate([taps(4), anti], 0).astype(BF16)))

    signal, end_signal, end_second, skip = [], [], [], []
    at_end = [lane == 0, lane == tok - 1]
    for c in range(2):
        ends = take(12 + c)
        prior = jnp.where(place == 0, 0.0, pltpu.roll(ends, 1, 0))
        after = jnp.where(place == chips - 1, 0.0, pltpu.roll(ends, chips - 1, 0))
        full = ends + left(jnp.where(lane % 2 == 1, after, prior), 6)
        end_signal.append(full * left(full, 2))
        end_second.append(left(full, 4))
        signal.append([jnp.where(at_end[h], end_signal[c], take(2 * h + c)) for h in range(2)])
        index = lax.broadcasted_iota(jnp.int32, skip_ref.shape, 1)
        skip.append(jnp.sum(jnp.where(index == owner + c, skip_ref[...], 0.0), 1, keepdims=True))
    x = jnp.concatenate([jnp.concatenate(part, 0) for part in signal], 1)
    s = spectrum(dot(table_ref[:, :blocks], x.astype(BF16)))

    real, imag = [], []
    for c in range(2):
        sr, si, fr, fi = s[c][:, :tok], s[c][:, tok:], f[c][:, :tok], f[c][:, tok:]
        y = jnp.concatenate([sr * fr - si * fi, sr * fi + si * fr], 1)
        g = dot(y.astype(BF16), table_ref[2 * tok : 4 * tok, inner])
        re, im = g[:, :tok], g[:, tok:]
        real.append(re * cos - im * sin)
        imag.append(re * sin + im * cos)
    e = jnp.concatenate([jnp.concatenate(real, 1), jnp.concatenate(imag, 1)], 0)
    out = dot(jnp.concatenate([table_ref[:blocks, back], table_ref[blocks : 2 * blocks, back]], 1), e.astype(BF16))
    for c in range(2):
        for h in range(2):
            conv = out[h * chips : (h + 1) * chips, c * tok : (c + 1) * tok] + skip[c] * signal[c][h]
            conv = jnp.where(at_end[h], end_second[c] * conv, conv)
            buf[pl.ds(2 * h + c, chips, stride=4), :] = conv
    out_ref[...] = buf[...].astype(BF16)


def last_kernel(conv_ref, second_ref, w_ref, out_ref, buf, sorted_ref):
    channels, rows = conv_ref.shape
    quarter = channels // 4
    buf[...] = conv_ref[...].astype(F32)
    for h in range(2):
        for c in range(2):
            sorted_ref[pl.ds(h * channels // 2 + c, quarter, stride=2), :] = buf[
                pl.ds(2 * h + c, quarter, stride=4), :
            ]
    conv = sorted_ref[...]
    lane = lax.broadcasted_iota(jnp.int32, conv.shape, 1)
    at_end = lane == lax.axis_index("fft") % 2 * (rows - 1)
    gated = jnp.where(at_end, conv, second_ref[...] * conv).astype(BF16)
    out_ref[...] = lax.dot_general(
        gated, w_ref[...], (((0,), (0,)), ((), ())), preferred_element_type=F32
    ).astype(BF16)


def call(kernel, outs, scratch=(), mib=24, cost=0, **specs):
    return pl.pallas_call(
        kernel,
        out_shape=outs,
        scratch_shapes=list(scratch),
        compiler_params=pltpu.CompilerParams(vmem_limit_bytes=mib * 1024 * 1024),
        cost_estimate=pl.CostEstimate(flops=cost, bytes_accessed=0, transcendentals=0) if cost else None,
        **specs,
    )


def exchange(x, groups=None):
    return lax.all_to_all(x, AXES, split_axis=0, concat_axis=0, axis_index_groups=groups, tiled=True)


def body(tokens, w_in, conv_taps, causal_taps, anticausal_taps, skip_gain, w_out):
    rows = tokens.shape[0]
    channels, width = w_out.shape
    count = lax.axis_size(AXES)
    shape = jax.ShapeDtypeStruct
    vmem = pltpu.VMEM
    table = tables(count, rows)

    mates = [(i, i ^ 1) for i in range(count)]
    tok_mate, causal_mate, anti_mate = [lax.ppermute(x, AXES, mates) for x in (tokens, causal_taps, anticausal_taps)]
    twist = call(first_kernel, shape((count, 2 * rows), F32), cost=2 * 10**9)()
    send, second = call(
        front_kernel,
        [shape((7 * count, rows), BF16), shape((channels, rows), F32)],
        [
            vmem((2 * rows, tokens.shape[1]), BF16),
            vmem((8, channels), F32),
            vmem((channels // 2, rows), F32),
            vmem((7 * count, rows), F32),
        ],
    )(twist, tokens, tok_mate, w_in, conv_taps, causal_taps, causal_mate, anticausal_taps, anti_mate)
    cores = [list(range(core, count, 2)) for core in range(2)]
    got = exchange(send.reshape(-1, 2, rows), cores).reshape(send.shape)

    conv = call(
        conv_kernel,
        shape((channels, rows), BF16),
        [vmem((channels, rows), F32), vmem((7 * count, rows), F32)],
    )(got, skip_gain[None], table, twist)
    conv = exchange(conv)
    return call(last_kernel, shape((rows, width), BF16), [vmem((channels, rows), F32)] * 2)(conv, second, w_out)


def solution(mesh):
    rows = P(AXES, None)
    in_specs = (rows, P(), P(), rows, rows, P(), P())
    return jax.shard_map(body, mesh=mesh, in_specs=in_specs, out_specs=rows, check_vma=False)
```

```python
import math

import jax
import jax.numpy as jnp
import numpy as np
from jax import lax
from jax.experimental import pallas as pl
from jax.experimental.pallas import tpu as pltpu
from jax.sharding import PartitionSpec as P

AXES = ("blk", "fft")
F32 = jnp.float32
BF16 = jnp.bfloat16
MESSAGE, ROW = 25, 3


def tables(blocks, tok):
    length = 2 * blocks * tok
    half = np.arange(blocks) + 0.5
    ang = 2 * math.pi * np.outer(half, np.arange(2 * blocks)) / (2 * blocks)
    fore = np.concatenate([np.cos(ang), -np.sin(ang)], 0)
    back = np.concatenate([fore[:blocks, :blocks].T, fore[blocks:, :blocks].T], 0) * (2 / length)
    fore[:, blocks:] *= -1
    inner = 2 * math.pi * np.outer(np.arange(tok), np.arange(tok)) / tok
    c, s = np.cos(inner), np.sin(inner)
    inner = np.block([[c, -s], [s, c], [c, s], [-s, c]])
    return jnp.asarray(np.concatenate([fore, inner, back], 1), BF16)


def dot(a, b):
    return jnp.dot(a, b, preferred_element_type=F32)


def first_kernel(twist_ref):
    blocks, tok = twist_ref.shape[0], twist_ref.shape[1] // 2
    k = lax.broadcasted_iota(jnp.int32, (blocks, tok), 0)
    t = lax.broadcasted_iota(jnp.int32, (blocks, tok), 1)
    angle = ((2 * k + 1) * t).astype(F32) * (math.pi / (2 * blocks * tok))
    twist_ref[:, :tok] = jnp.cos(angle)
    twist_ref[:, tok:] = jnp.sin(angle)


def front_kernel(
    _, tok_ref, w_ref, taps_ref, skip_ref, causal_ref, anti_ref,
    send_ref, second_ref, direct_ref, buf, wide,
):
    rows = tok_ref.shape[0]
    channels = causal_ref.shape[1]
    half = channels // 2
    row = lax.broadcasted_iota(jnp.int32, (rows, channels), 0)

    def slab(i):
        return slice(i * channels, (i + 1) * channels)

    def place(a, block):
        buf[...] = block.T
        for c in range(2):
            wide[pl.ds(ROW * (2 * a + c), half, stride=MESSAGE), :] = buf[pl.ds(c, half, stride=2), :]

    def short(i):
        proj = dot(tok_ref[...], w_ref[:, slab(i)]).astype(BF16).astype(F32)
        prior, here, after = [taps_ref[k : k + 1, slab(i)] for k in range(3)]
        up = jnp.where(row == 0, 0.0, pltpu.roll(proj, 1, 0))
        down = jnp.where(row == rows - 1, 0.0, pltpu.roll(proj, rows - 1, 0))
        return prior * up + here * proj + after * down, after * proj[:1], prior * proj[rows - 1 :]

    place(1, causal_ref[...].astype(F32))
    place(2, anti_ref[...].astype(F32))
    first, first_up, first_down = short(0)
    value, value_up, value_down = short(2)
    signal = first * value
    place(0, signal)
    direct_ref[...] = (skip_ref[...] * signal).T
    second, second_up, second_down = short(1)
    second_ref[...] = second.T
    last = rows - 1
    ends = [
        first[:1], value[last:], value[:1], second[last:], second[:1],
        first_up, first_down, value_up, value_down, second_up, second_down,
        skip_ref[...], skip_ref[...],
    ]
    fill = jnp.zeros((rows - len(ends) - 1, channels), F32)
    place(3, jnp.concatenate(ends + [fill, first[last:]], 0))
    for i in range(0, half, 2):
        pair = [wide[pl.ds(MESSAGE * (i + k), 8, stride=ROW), :] for k in range(2)]
        send_ref[8 * i : 8 * i + 16, :] = jnp.concatenate(pair, 0).astype(BF16)


def conv_kernel(got_ref, table_ref, twist_ref, out_ref, buf, wide):
    tok = got_ref.shape[1]
    blocks = got_ref.shape[0] // 8
    cos, sin = twist_ref[:, :tok], twist_ref[:, tok:]
    inner = slice(2 * blocks, 2 * blocks + 2 * tok)
    back = slice(2 * blocks + 2 * tok, 3 * blocks + 2 * tok)
    place = lax.broadcasted_iota(jnp.int32, (blocks, tok), 0)
    lane = lax.broadcasted_iota(jnp.int32, (blocks, tok), 1)
    at_end = (lane == 0) | (lane == tok - 1)

    def left(x, n):
        return pltpu.roll(x, tok - n, 1)

    def take(a, c):
        return wide[pl.ds(ROW * (2 * a + c), blocks, stride=MESSAGE), :]

    def spectrum(b):
        parts = []
        for c in range(2):
            lanes = slice(c * tok, (c + 1) * tok)
            re, im = b[:blocks, lanes], b[blocks:, lanes]
            parts.append(jnp.concatenate([re * cos + im * sin, im * cos - re * sin], 1))
        return [dot(part.astype(BF16), table_ref[: 2 * tok, inner]) for part in parts]

    got = got_ref[...].astype(F32)
    for i in range(blocks):
        wide[pl.ds(MESSAGE * i, 8, stride=ROW), :] = got[8 * i : 8 * i + 8]
    causal = jnp.concatenate([take(1, 0), take(1, 1)], 1)
    anti = jnp.concatenate(
        [jnp.where((place == 0) & (lane == 0), 0.0, take(2, c)) for c in range(2)], 1
    )
    f = spectrum(dot(table_ref[:, : 2 * blocks], jnp.concatenate([causal, anti], 0).astype(BF16)))

    signal, end_signal, end_second, end_skip = [], [], [], []
    for c in range(2):
        ends = take(3, c)
        prior = jnp.where(place == 0, 0.0, pltpu.roll(ends, 1, 0))
        after = jnp.where(place == blocks - 1, 0.0, pltpu.roll(ends, blocks - 1, 0))
        full = ends + left(jnp.where(lane % 2 == 1, after, prior), 6)
        end_signal.append(full * left(full, 2))
        end_second.append(left(full, 4))
        end_skip.append(left(ends, 12))
        signal.append(jnp.where(at_end, end_signal[c], take(0, c)))
    s = spectrum(dot(table_ref[:, :blocks], jnp.concatenate(signal, 1).astype(BF16)))

    real, imag = [], []
    for c in range(2):
        sr, si, fr, fi = s[c][:, :tok], s[c][:, tok:], f[c][:, :tok], f[c][:, tok:]
        y = jnp.concatenate([sr * fr - si * fi, sr * fi + si * fr], 1)
        g = dot(y.astype(BF16), table_ref[2 * tok : 4 * tok, inner])
        re, im = g[:, :tok], g[:, tok:]
        real.append(re * cos - im * sin)
        imag.append(re * sin + im * cos)
    e = jnp.concatenate([jnp.concatenate(real, 1), jnp.concatenate(imag, 1)], 0)
    out = dot(jnp.concatenate([table_ref[:blocks, back], table_ref[blocks : 2 * blocks, back]], 1), e.astype(BF16))
    for c in range(2):
        conv = out[:, c * tok : (c + 1) * tok]
        gated = end_second[c] * (conv + end_skip[c] * end_signal[c])
        buf[pl.ds(c, blocks, stride=2), :] = jnp.where(at_end, gated, conv)
    out_ref[...] = buf[...].astype(BF16)


def last_kernel(conv_ref, second_ref, direct_ref, w_ref, out_ref):
    conv = conv_ref[...].astype(F32)
    lane = lax.broadcasted_iota(jnp.int32, conv.shape, 1)
    at_end = (lane == 0) | (lane == conv.shape[1] - 1)
    gated = jnp.where(at_end, conv, second_ref[...] * (conv + direct_ref[...])).astype(BF16)
    out_ref[...] = lax.dot_general(
        gated, w_ref[...], (((0,), (0,)), ((), ())), preferred_element_type=F32
    ).astype(BF16)


def call(kernel, outs, scratch=(), mib=24, cost=0, **specs):
    return pl.pallas_call(
        kernel,
        out_shape=outs,
        scratch_shapes=list(scratch),
        compiler_params=pltpu.CompilerParams(vmem_limit_bytes=mib * 1024 * 1024),
        cost_estimate=pl.CostEstimate(flops=cost, bytes_accessed=0, transcendentals=0) if cost else None,
        **specs,
    )


def exchange(x):
    return lax.all_to_all(x, AXES, split_axis=0, concat_axis=0, tiled=True)


def body(tokens, w_in, conv_taps, causal_taps, anticausal_taps, skip_gain, w_out):
    rows = tokens.shape[0]
    channels, width = w_out.shape
    count = lax.axis_size(AXES)
    shape = jax.ShapeDtypeStruct
    vmem = pltpu.VMEM
    table = tables(count, rows)

    staged = (tokens, w_in, conv_taps, skip_gain[None], causal_taps, anticausal_taps)
    twist = call(first_kernel, shape((count, 2 * rows), F32), cost=2 * 10**9)()
    send, second, direct = call(
        front_kernel,
        [shape((4 * channels, rows), BF16), shape((channels, rows), F32), shape((channels, rows), F32)],
        [vmem((channels, rows), F32), vmem((MESSAGE * (count + 1), rows), F32)],
    )(twist, *staged)
    got = exchange(send.reshape(count, 8, rows)).reshape(send.shape)

    conv = call(
        conv_kernel,
        shape((channels, rows), BF16),
        [vmem((channels, rows), F32), vmem((MESSAGE * (count + 1), rows), F32)],
    )(got, table, twist)
    conv = exchange(conv)
    return call(last_kernel, shape((rows, width), BF16))(conv, second, direct, w_out)


def solution(mesh):
    rows = P(AXES, None)
    in_specs = (rows, P(), P(), rows, rows, P(), P())
    return jax.shard_map(body, mesh=mesh, in_specs=in_specs, out_specs=rows, check_vma=False)
```

```python
import math

import jax
import jax.numpy as jnp
import numpy as np
from jax import lax
from jax.experimental import pallas as pl
from jax.experimental.pallas import tpu as pltpu
from jax.sharding import PartitionSpec as P

AXES = ("blk", "fft")
F32 = jnp.float32
BF16 = jnp.bfloat16
MESSAGE, ROW = 25, 3


def tables(blocks, tok):
    length = 2 * blocks * tok
    half = np.arange(blocks) + 0.5
    ang = 2 * math.pi * np.outer(half, np.arange(2 * blocks)) / (2 * blocks)
    fore = np.concatenate([np.cos(ang), -np.sin(ang)], 0)
    back = np.concatenate([fore[:blocks, :blocks].T, fore[blocks:, :blocks].T], 0) * (2 / length)
    fore[:, blocks:] *= -1
    inner = 2 * math.pi * np.outer(np.arange(tok), np.arange(tok)) / tok
    c, s = np.cos(inner), np.sin(inner)
    inner = np.block([[c, -s], [s, c], [c, s], [-s, c]])
    return jnp.asarray(np.concatenate([fore, inner, back], 1), BF16)


def dot(a, b):
    return jnp.dot(a, b, preferred_element_type=F32)


def first_kernel(twist_ref):
    blocks, tok = twist_ref.shape[0], twist_ref.shape[1] // 2
    k = lax.broadcasted_iota(jnp.int32, (blocks, tok), 0)
    t = lax.broadcasted_iota(jnp.int32, (blocks, tok), 1)
    angle = ((2 * k + 1) * t).astype(F32) * (math.pi / (2 * blocks * tok))
    twist_ref[:, :tok] = jnp.cos(angle)
    twist_ref[:, tok:] = jnp.sin(angle)


def front_kernel(
    _, tok_ref, w_ref, taps_ref, causal_ref, anti_ref,
    send_ref, second_ref, buf, wide,
):
    rows = tok_ref.shape[0]
    channels = causal_ref.shape[1]
    half = channels // 2
    row = lax.broadcasted_iota(jnp.int32, (rows, channels), 0)

    def slab(i):
        return slice(i * channels, (i + 1) * channels)

    def place(a, block):
        buf[...] = block.T
        for c in range(2):
            wide[pl.ds(ROW * (2 * a + c), half, stride=MESSAGE), :] = buf[pl.ds(c, half, stride=2), :]

    def short(i):
        proj = dot(tok_ref[...], w_ref[:, slab(i)]).astype(BF16).astype(F32)
        prior, here, after = [taps_ref[k : k + 1, slab(i)] for k in range(3)]
        up = jnp.where(row == 0, 0.0, pltpu.roll(proj, 1, 0))
        down = jnp.where(row == rows - 1, 0.0, pltpu.roll(proj, rows - 1, 0))
        return prior * up + here * proj + after * down, after * proj[:1], prior * proj[rows - 1 :]

    place(1, causal_ref[...].astype(F32))
    place(2, anti_ref[...].astype(F32))
    first, first_up, first_down = short(0)
    value, value_up, value_down = short(2)
    signal = first * value
    place(0, signal)
    second, second_up, second_down = short(1)
    second_ref[...] = second.T
    last = rows - 1
    ends = [
        first[:1], value[last:], value[:1], second[last:], second[:1],
        first_up, first_down, value_up, value_down, second_up, second_down,
    ]
    fill = jnp.zeros((rows - len(ends) - 1, channels), F32)
    place(3, jnp.concatenate(ends + [fill, first[last:]], 0))
    for i in range(0, half, 2):
        pair = [wide[pl.ds(MESSAGE * (i + k), 8, stride=ROW), :] for k in range(2)]
        send_ref[8 * i : 8 * i + 16, :] = jnp.concatenate(pair, 0).astype(BF16)


def conv_kernel(got_ref, skip_ref, table_ref, twist_ref, out_ref, buf, wide):
    tok = got_ref.shape[1]
    blocks = got_ref.shape[0] // 8
    cos, sin = twist_ref[:, :tok], twist_ref[:, tok:]
    inner = slice(2 * blocks, 2 * blocks + 2 * tok)
    back = slice(2 * blocks + 2 * tok, 3 * blocks + 2 * tok)
    place = lax.broadcasted_iota(jnp.int32, (blocks, tok), 0)
    lane = lax.broadcasted_iota(jnp.int32, (blocks, tok), 1)
    at_end = (lane == 0) | (lane == tok - 1)

    def left(x, n):
        return pltpu.roll(x, tok - n, 1)

    def take(a, c):
        return wide[pl.ds(ROW * (2 * a + c), blocks, stride=MESSAGE), :]

    def spectrum(b):
        parts = []
        for c in range(2):
            lanes = slice(c * tok, (c + 1) * tok)
            re, im = b[0][:, lanes], b[1][:, lanes]
            parts.append(jnp.concatenate([re * cos + im * sin, im * cos - re * sin], 1))
        return [dot(part.astype(BF16), table_ref[: 2 * tok, inner]) for part in parts]

    got = got_ref[...].astype(F32)
    for i in range(blocks):
        wide[pl.ds(MESSAGE * i, 8, stride=ROW), :] = got[8 * i : 8 * i + 8]
    causal = jnp.concatenate([take(1, 0), take(1, 1)], 1)
    anti = jnp.concatenate(
        [jnp.where((place == 0) & (lane == 0), 0.0, take(2, c)) for c in range(2)], 1
    )
    taps = jnp.concatenate([causal, anti], 0).astype(BF16)
    f = spectrum([dot(table_ref[i * blocks : (i + 1) * blocks, : 2 * blocks], taps) for i in range(2)])

    signal, end_second, skip = [], [], []
    device = lax.axis_index("blk") * lax.axis_size("fft") + lax.axis_index("fft")
    channel = lax.broadcasted_iota(jnp.int32, skip_ref.shape, 1)
    for c in range(2):
        ends = take(3, c)
        prior = jnp.where(place == 0, 0.0, pltpu.roll(ends, 1, 0))
        after = jnp.where(place == blocks - 1, 0.0, pltpu.roll(ends, blocks - 1, 0))
        full = ends + left(jnp.where(lane % 2 == 1, after, prior), 6)
        end_second.append(left(full, 4))
        signal.append(jnp.where(at_end, full * left(full, 2), take(0, c)))
        skip.append(jnp.sum(jnp.where(channel == 2 * device + c, skip_ref[...], 0.0), 1, keepdims=True))
    x = jnp.concatenate(signal, 1).astype(BF16)
    s = spectrum([dot(table_ref[i * blocks : (i + 1) * blocks, :blocks], x) for i in range(2)])

    real, imag = [], []
    for c in range(2):
        sr, si, fr, fi = s[c][:, :tok], s[c][:, tok:], f[c][:, :tok], f[c][:, tok:]
        y = jnp.concatenate([sr * fr - si * fi, sr * fi + si * fr], 1)
        g = dot(y.astype(BF16), table_ref[2 * tok : 4 * tok, inner])
        re, im = g[:, :tok], g[:, tok:]
        real.append(re * cos - im * sin)
        imag.append(re * sin + im * cos)
    e = jnp.concatenate([jnp.concatenate(real, 1), jnp.concatenate(imag, 1)], 0)
    out = dot(jnp.concatenate([table_ref[:blocks, back], table_ref[blocks : 2 * blocks, back]], 1), e.astype(BF16))
    for c in range(2):
        conv = out[:, c * tok : (c + 1) * tok] + skip[c] * signal[c]
        buf[pl.ds(c, blocks, stride=2), :] = jnp.where(at_end, end_second[c] * conv, conv)
    out_ref[...] = buf[...].astype(BF16)


def last_kernel(conv_ref, second_ref, w_ref, out_ref):
    conv = conv_ref[...].astype(F32)
    lane = lax.broadcasted_iota(jnp.int32, conv.shape, 1)
    at_end = (lane == 0) | (lane == conv.shape[1] - 1)
    gated = jnp.where(at_end, conv, second_ref[...] * conv).astype(BF16)
    out_ref[...] = lax.dot_general(
        gated, w_ref[...], (((0,), (0,)), ((), ())), preferred_element_type=F32
    ).astype(BF16)


def call(kernel, outs, scratch=(), mib=24, cost=0, **specs):
    return pl.pallas_call(
        kernel,
        out_shape=outs,
        scratch_shapes=list(scratch),
        compiler_params=pltpu.CompilerParams(vmem_limit_bytes=mib * 1024 * 1024),
        cost_estimate=pl.CostEstimate(flops=cost, bytes_accessed=0, transcendentals=0) if cost else None,
        **specs,
    )


def exchange(x):
    return lax.all_to_all(x, AXES, split_axis=0, concat_axis=0, tiled=True)


def body(tokens, w_in, conv_taps, causal_taps, anticausal_taps, skip_gain, w_out):
    rows = tokens.shape[0]
    channels, width = w_out.shape
    count = lax.axis_size(AXES)
    shape = jax.ShapeDtypeStruct
    vmem = pltpu.VMEM
    table = tables(count, rows)

    staged = (tokens, w_in, conv_taps, causal_taps, anticausal_taps)
    twist = call(first_kernel, shape((count, 2 * rows), F32), cost=2 * 10**9)()
    send, second = call(
        front_kernel,
        [shape((4 * channels, rows), BF16), shape((channels, rows), F32)],
        [vmem((channels, rows), F32), vmem((MESSAGE * (count + 1), rows), F32)],
    )(twist, *staged)
    got = exchange(send.reshape(count, 8, rows)).reshape(send.shape)

    conv = call(
        conv_kernel,
        shape((channels, rows), BF16),
        [vmem((channels, rows), F32), vmem((MESSAGE * (count + 1), rows), F32)],
    )(got, skip_gain[None], table, twist)
    conv = exchange(conv)
    return call(last_kernel, shape((rows, width), BF16))(conv, second, w_out)


def solution(mesh):
    rows = P(AXES, None)
    in_specs = (rows, P(), P(), rows, rows, P(), P())
    return jax.shard_map(body, mesh=mesh, in_specs=in_specs, out_specs=rows, check_vma=False)
```

```python
import math

import jax
import jax.numpy as jnp
import numpy as np
from jax import lax
from jax.experimental import pallas as pl
from jax.experimental.pallas import tpu as pltpu
from jax.sharding import PartitionSpec as P

AXES = ("blk", "fft")
F32 = jnp.float32
BF16 = jnp.bfloat16
MESSAGE, ROW = 25, 3


def tables(blocks, tok):
    length = 2 * blocks * tok
    half = np.arange(blocks) + 0.5
    ang = 2 * math.pi * np.outer(half, np.arange(2 * blocks)) / (2 * blocks)
    fore = np.concatenate([np.cos(ang), -np.sin(ang)], 0)
    back = np.concatenate([fore[:blocks, :blocks].T, fore[blocks:, :blocks].T], 0) * (2 / length)
    fore[:, blocks:] *= -1
    inner = 2 * math.pi * np.outer(np.arange(tok), np.arange(tok)) / tok
    c, s = np.cos(inner), np.sin(inner)
    inner = np.block([[c, -s], [s, c], [c, s], [-s, c]])
    return jnp.asarray(np.concatenate([fore, inner, back], 1), BF16)


def dot(a, b):
    return jnp.dot(a, b, preferred_element_type=F32)


def first_kernel(twist_ref):
    blocks, tok = twist_ref.shape[0], twist_ref.shape[1] // 2
    k = lax.broadcasted_iota(jnp.int32, (blocks, tok), 0)
    t = lax.broadcasted_iota(jnp.int32, (blocks, tok), 1)
    angle = ((2 * k + 1) * t).astype(F32) * (math.pi / (2 * blocks * tok))
    twist_ref[:, :tok] = jnp.cos(angle)
    twist_ref[:, tok:] = jnp.sin(angle)


def front_kernel(
    _, tok_ref, w_ref, taps_ref, skip_ref, causal_ref, anti_ref,
    send_ref, second_ref, direct_ref, buf, wide,
):
    rows = tok_ref.shape[0]
    channels = causal_ref.shape[1]
    half = channels // 2
    row = lax.broadcasted_iota(jnp.int32, (rows, channels), 0)

    def slab(i):
        return slice(i * channels, (i + 1) * channels)

    def place(a, block):
        buf[...] = block.T
        for c in range(2):
            wide[pl.ds(ROW * (2 * a + c), half, stride=MESSAGE), :] = buf[pl.ds(c, half, stride=2), :]

    def short(i):
        proj = dot(tok_ref[...], w_ref[:, slab(i)]).astype(BF16).astype(F32)
        prior, here, after = [taps_ref[k : k + 1, slab(i)] for k in range(3)]
        up = jnp.where(row == 0, 0.0, pltpu.roll(proj, 1, 0))
        down = jnp.where(row == rows - 1, 0.0, pltpu.roll(proj, rows - 1, 0))
        return prior * up + here * proj + after * down, after * proj[:1], prior * proj[rows - 1 :]

    place(1, causal_ref[...].astype(F32))
    place(2, anti_ref[...].astype(F32))
    first, first_up, first_down = short(0)
    value, value_up, value_down = short(2)
    signal = first * value
    place(0, signal)
    direct_ref[...] = (skip_ref[...] * signal).T
    second, second_up, second_down = short(1)
    second_ref[...] = second.T
    last = rows - 1
    ends = [
        first[:1], value[last:], value[:1], second[last:], second[:1],
        first_up, first_down, value_up, value_down, second_up, second_down,
        skip_ref[...], skip_ref[...],
    ]
    fill = jnp.zeros((rows - len(ends) - 1, channels), F32)
    place(3, jnp.concatenate(ends + [fill, first[last:]], 0))
    for i in range(0, half, 2):
        pair = [wide[pl.ds(MESSAGE * (i + k), 8, stride=ROW), :] for k in range(2)]
        send_ref[8 * i : 8 * i + 16, :] = jnp.concatenate(pair, 0).astype(BF16)


def conv_kernel(got_ref, table_ref, twist_ref, out_ref, buf, wide):
    tok = got_ref.shape[1]
    blocks = got_ref.shape[0] // 8
    cos, sin = twist_ref[:, :tok], twist_ref[:, tok:]
    inner = slice(2 * blocks, 2 * blocks + 2 * tok)
    back = slice(2 * blocks + 2 * tok, 3 * blocks + 2 * tok)
    place = lax.broadcasted_iota(jnp.int32, (blocks, tok), 0)
    lane = lax.broadcasted_iota(jnp.int32, (blocks, tok), 1)
    at_end = (lane == 0) | (lane == tok - 1)

    def left(x, n):
        return pltpu.roll(x, tok - n, 1)

    def take(a, c):
        return wide[pl.ds(ROW * (2 * a + c), blocks, stride=MESSAGE), :]

    def spectrum(b):
        parts = []
        for c in range(2):
            lanes = slice(c * tok, (c + 1) * tok)
            re, im = b[0][:, lanes], b[1][:, lanes]
            parts.append(jnp.concatenate([re * cos + im * sin, im * cos - re * sin], 1))
        return [dot(part.astype(BF16), table_ref[: 2 * tok, inner]) for part in parts]

    got = got_ref[...].astype(F32)
    for i in range(blocks):
        wide[pl.ds(MESSAGE * i, 8, stride=ROW), :] = got[8 * i : 8 * i + 8]
    causal = jnp.concatenate([take(1, 0), take(1, 1)], 1)
    anti = jnp.concatenate(
        [jnp.where((place == 0) & (lane == 0), 0.0, take(2, c)) for c in range(2)], 1
    )
    taps = jnp.concatenate([causal, anti], 0).astype(BF16)
    f = spectrum([dot(table_ref[i * blocks : (i + 1) * blocks, : 2 * blocks], taps) for i in range(2)])

    signal, end_signal, end_second, end_skip = [], [], [], []
    for c in range(2):
        ends = take(3, c)
        prior = jnp.where(place == 0, 0.0, pltpu.roll(ends, 1, 0))
        after = jnp.where(place == blocks - 1, 0.0, pltpu.roll(ends, blocks - 1, 0))
        full = ends + left(jnp.where(lane % 2 == 1, after, prior), 6)
        end_signal.append(full * left(full, 2))
        end_second.append(left(full, 4))
        end_skip.append(left(ends, 12))
        signal.append(jnp.where(at_end, end_signal[c], take(0, c)))
    x = jnp.concatenate(signal, 1).astype(BF16)
    s = spectrum([dot(table_ref[i * blocks : (i + 1) * blocks, :blocks], x) for i in range(2)])

    real, imag = [], []
    for c in range(2):
        sr, si, fr, fi = s[c][:, :tok], s[c][:, tok:], f[c][:, :tok], f[c][:, tok:]
        y = jnp.concatenate([sr * fr - si * fi, sr * fi + si * fr], 1)
        g = dot(y.astype(BF16), table_ref[2 * tok : 4 * tok, inner])
        re, im = g[:, :tok], g[:, tok:]
        real.append(re * cos - im * sin)
        imag.append(re * sin + im * cos)
    e = jnp.concatenate([jnp.concatenate(real, 1), jnp.concatenate(imag, 1)], 0)
    out = dot(jnp.concatenate([table_ref[:blocks, back], table_ref[blocks : 2 * blocks, back]], 1), e.astype(BF16))
    for c in range(2):
        conv = out[:, c * tok : (c + 1) * tok]
        gated = end_second[c] * (conv + end_skip[c] * end_signal[c])
        buf[pl.ds(c, blocks, stride=2), :] = jnp.where(at_end, gated, conv)
    out_ref[...] = buf[...].astype(BF16)


def last_kernel(conv_ref, second_ref, direct_ref, w_ref, out_ref):
    conv = conv_ref[...].astype(F32)
    lane = lax.broadcasted_iota(jnp.int32, conv.shape, 1)
    at_end = (lane == 0) | (lane == conv.shape[1] - 1)
    gated = jnp.where(at_end, conv, second_ref[...] * (conv + direct_ref[...])).astype(BF16)
    out_ref[...] = lax.dot_general(
        gated, w_ref[...], (((0,), (0,)), ((), ())), preferred_element_type=F32
    ).astype(BF16)


def call(kernel, outs, scratch=(), mib=24, cost=0, **specs):
    return pl.pallas_call(
        kernel,
        out_shape=outs,
        scratch_shapes=list(scratch),
        compiler_params=pltpu.CompilerParams(vmem_limit_bytes=mib * 1024 * 1024),
        cost_estimate=pl.CostEstimate(flops=cost, bytes_accessed=0, transcendentals=0) if cost else None,
        **specs,
    )


def exchange(x):
    return lax.all_to_all(x, AXES, split_axis=0, concat_axis=0, tiled=True)


def body(tokens, w_in, conv_taps, causal_taps, anticausal_taps, skip_gain, w_out):
    rows = tokens.shape[0]
    channels, width = w_out.shape
    count = lax.axis_size(AXES)
    shape = jax.ShapeDtypeStruct
    vmem = pltpu.VMEM
    table = tables(count, rows)

    staged = (tokens, w_in, conv_taps, skip_gain[None], causal_taps, anticausal_taps)
    twist = call(first_kernel, shape((count, 2 * rows), F32), cost=2 * 10**9)()
    send, second, direct = call(
        front_kernel,
        [shape((4 * channels, rows), BF16), shape((channels, rows), F32), shape((channels, rows), F32)],
        [vmem((channels, rows), F32), vmem((MESSAGE * (count + 1), rows), F32)],
    )(twist, *staged)
    got = exchange(send.reshape(count, 8, rows)).reshape(send.shape)

    conv = call(
        conv_kernel,
        shape((channels, rows), BF16),
        [vmem((channels, rows), F32), vmem((MESSAGE * (count + 1), rows), F32)],
    )(got, table, twist)
    conv = exchange(conv)
    return call(last_kernel, shape((rows, width), BF16))(conv, second, direct, w_out)


def solution(mesh):
    rows = P(AXES, None)
    in_specs = (rows, P(), P(), rows, rows, P(), P())
    return jax.shard_map(body, mesh=mesh, in_specs=in_specs, out_specs=rows, check_vma=False)
```

```python
import math

import jax
import jax.numpy as jnp
import numpy as np
from jax import lax
from jax.experimental import pallas as pl
from jax.experimental.pallas import tpu as pltpu
from jax.sharding import PartitionSpec as P

AXES = ("blk", "fft")
F32 = jnp.float32
BF16 = jnp.bfloat16
MESSAGE, ROW = 25, 3


def tables(blocks, tok):
    length = 2 * blocks * tok
    half = np.arange(blocks) + 0.5
    ang = 2 * math.pi * np.outer(half, np.arange(2 * blocks)) / (2 * blocks)
    fore = np.concatenate([np.cos(ang), -np.sin(ang)], 0)
    back = np.concatenate([fore[:blocks, :blocks].T, fore[blocks:, :blocks].T], 0) * (2 / length)
    fore[:, blocks:] *= -1
    inner = 2 * math.pi * np.outer(np.arange(tok), np.arange(tok)) / tok
    c, s = np.cos(inner), np.sin(inner)
    inner = np.block([[c, -s], [s, c], [c, s], [-s, c]])
    return jnp.asarray(np.concatenate([fore, inner, back], 1), BF16)


def dot(a, b):
    return jnp.dot(a, b, preferred_element_type=F32)


def first_kernel(twist_ref):
    blocks, tok = twist_ref.shape[0], twist_ref.shape[1] // 2
    k = lax.broadcasted_iota(jnp.int32, (blocks, tok), 0)
    t = lax.broadcasted_iota(jnp.int32, (blocks, tok), 1)
    angle = ((2 * k + 1) * t).astype(F32) * (math.pi / (2 * blocks * tok))
    twist_ref[:, :tok] = jnp.cos(angle)
    twist_ref[:, tok:] = jnp.sin(angle)


def front_kernel(
    _, tok_ref, w_ref, taps_ref, skip_ref, causal_ref, anti_ref,
    send_ref, second_ref, direct_ref, buf, wide,
):
    rows = tok_ref.shape[0]
    channels = causal_ref.shape[1]
    half = channels // 2
    row = lax.broadcasted_iota(jnp.int32, (rows, channels), 0)

    def slab(i):
        return slice(i * channels, (i + 1) * channels)

    def place(a, block):
        buf[...] = block.T
        for c in range(2):
            wide[pl.ds(ROW * (2 * a + c), half, stride=MESSAGE), :] = buf[pl.ds(c, half, stride=2), :]

    def short(i):
        proj = dot(tok_ref[...], w_ref[:, slab(i)]).astype(BF16).astype(F32)
        prior, here, after = [taps_ref[k : k + 1, slab(i)] for k in range(3)]
        up = jnp.where(row == 0, 0.0, pltpu.roll(proj, 1, 0))
        down = jnp.where(row == rows - 1, 0.0, pltpu.roll(proj, rows - 1, 0))
        return prior * up + here * proj + after * down, after * proj[:1], prior * proj[rows - 1 :]

    place(1, causal_ref[...].astype(F32))
    place(2, anti_ref[...].astype(F32))
    first, first_up, first_down = short(0)
    value, value_up, value_down = short(2)
    signal = first * value
    place(0, signal)
    direct_ref[...] = (skip_ref[...] * signal).T
    second, second_up, second_down = short(1)
    second_ref[...] = second.T
    last = rows - 1
    ends = [
        first[:1], value[last:], value[:1], second[last:], second[:1],
        first_up, first_down, value_up, value_down, second_up, second_down,
        skip_ref[...], skip_ref[...],
    ]
    fill = jnp.zeros((rows - len(ends) - 1, channels), F32)
    place(3, jnp.concatenate(ends + [fill, first[last:]], 0))
    for i in range(0, half, 2):
        pair = [wide[pl.ds(MESSAGE * (i + k), 8, stride=ROW), :] for k in range(2)]
        send_ref[8 * i : 8 * i + 16, :] = jnp.concatenate(pair, 0).astype(BF16)


def conv_kernel(got_ref, table_ref, twist_ref, out_ref, buf, wide):
    tok = got_ref.shape[1]
    blocks = got_ref.shape[0] // 8
    cos, sin = twist_ref[:, :tok], twist_ref[:, tok:]
    inner = slice(2 * blocks, 2 * blocks + 2 * tok)
    back = slice(2 * blocks + 2 * tok, 3 * blocks + 2 * tok)
    place = lax.broadcasted_iota(jnp.int32, (blocks, tok), 0)
    lane = lax.broadcasted_iota(jnp.int32, (blocks, tok), 1)
    at_end = (lane == 0) | (lane == tok - 1)

    def left(x, n):
        return pltpu.roll(x, tok - n, 1)

    def take(a, c):
        return wide[pl.ds(ROW * (2 * a + c), blocks, stride=MESSAGE), :]

    def spectrum(b):
        parts = []
        for c in range(2):
            lanes = slice(c * tok, (c + 1) * tok)
            re, im = b[0][:, lanes], b[1][:, lanes]
            parts.append(jnp.concatenate([re * cos + im * sin, im * cos - re * sin], 1))
        return [dot(part.astype(BF16), table_ref[: 2 * tok, inner]) for part in parts]

    got = got_ref[...].astype(F32)
    for i in range(blocks):
        wide[pl.ds(MESSAGE * i, 8, stride=ROW), :] = got[8 * i : 8 * i + 8]
    causal = jnp.concatenate([take(1, 0), take(1, 1)], 1)
    anti = jnp.concatenate(
        [jnp.where((place == 0) & (lane == 0), 0.0, take(2, c)) for c in range(2)], 1
    )
    taps = jnp.concatenate([causal, anti], 0).astype(BF16)
    f = spectrum([dot(table_ref[i * blocks : (i + 1) * blocks, : 2 * blocks], taps) for i in range(2)])

    signal, end_signal, end_second, end_skip = [], [], [], []
    for c in range(2):
        ends = take(3, c)
        prior = jnp.where(place == 0, 0.0, pltpu.roll(ends, 1, 0))
        after = jnp.where(place == blocks - 1, 0.0, pltpu.roll(ends, blocks - 1, 0))
        full = ends + left(jnp.where(lane % 2 == 1, after, prior), 6)
        end_signal.append(full * left(full, 2))
        end_second.append(left(full, 4))
        end_skip.append(left(ends, 12))
        signal.append(jnp.where(at_end, end_signal[c], take(0, c)))
    x = jnp.concatenate(signal, 1).astype(BF16)
    s = spectrum([dot(table_ref[i * blocks : (i + 1) * blocks, :blocks], x) for i in range(2)])

    real, imag = [], []
    for c in range(2):
        sr, si, fr, fi = s[c][:, :tok], s[c][:, tok:], f[c][:, :tok], f[c][:, tok:]
        y = jnp.concatenate([sr * fr - si * fi, sr * fi + si * fr], 1)
        g = dot(y.astype(BF16), table_ref[2 * tok : 4 * tok, inner])
        re, im = g[:, :tok], g[:, tok:]
        real.append(re * cos - im * sin)
        imag.append(re * sin + im * cos)
    e = jnp.concatenate([jnp.concatenate(real, 1), jnp.concatenate(imag, 1)], 0)
    e = e.astype(BF16)
    rows = [
        jnp.concatenate([table_ref[k : k + tok, back], table_ref[blocks + k : blocks + k + tok, back]], 1)
        for k in range(0, blocks, tok)
    ]
    out = jnp.concatenate([dot(r, e) for r in rows], 0)
    for c in range(2):
        conv = out[:, c * tok : (c + 1) * tok]
        gated = end_second[c] * (conv + end_skip[c] * end_signal[c])
        buf[pl.ds(c, blocks, stride=2), :] = jnp.where(at_end, gated, conv)
    out_ref[...] = buf[...].astype(BF16)


def last_kernel(conv_ref, second_ref, direct_ref, w_ref, out_ref):
    conv = conv_ref[...].astype(F32)
    lane = lax.broadcasted_iota(jnp.int32, conv.shape, 1)
    at_end = (lane == 0) | (lane == conv.shape[1] - 1)
    gated = jnp.where(at_end, conv, second_ref[...] * (conv + direct_ref[...])).astype(BF16)
    out_ref[...] = lax.dot_general(
        gated, w_ref[...], (((0,), (0,)), ((), ())), preferred_element_type=F32
    ).astype(BF16)


def call(kernel, outs, scratch=(), mib=24, cost=0, **specs):
    return pl.pallas_call(
        kernel,
        out_shape=outs,
        scratch_shapes=list(scratch),
        compiler_params=pltpu.CompilerParams(vmem_limit_bytes=mib * 1024 * 1024),
        cost_estimate=pl.CostEstimate(flops=cost, bytes_accessed=0, transcendentals=0) if cost else None,
        **specs,
    )


def exchange(x):
    return lax.all_to_all(x, AXES, split_axis=0, concat_axis=0, tiled=True)


def body(tokens, w_in, conv_taps, causal_taps, anticausal_taps, skip_gain, w_out):
    rows = tokens.shape[0]
    channels, width = w_out.shape
    count = lax.axis_size(AXES)
    shape = jax.ShapeDtypeStruct
    vmem = pltpu.VMEM
    table = tables(count, rows)

    staged = (tokens, w_in, conv_taps, skip_gain[None], causal_taps, anticausal_taps)
    twist = call(first_kernel, shape((count, 2 * rows), F32), cost=2 * 10**9)()
    send, second, direct = call(
        front_kernel,
        [shape((4 * channels, rows), BF16), shape((channels, rows), F32), shape((channels, rows), F32)],
        [vmem((channels, rows), F32), vmem((MESSAGE * (count + 1), rows), F32)],
    )(twist, *staged)
    got = exchange(send.reshape(count, 8, rows)).reshape(send.shape)

    conv = call(
        conv_kernel,
        shape((channels, rows), BF16),
        [vmem((channels, rows), F32), vmem((MESSAGE * (count + 1), rows), F32)],
    )(got, table, twist)
    conv = exchange(conv)
    return call(last_kernel, shape((rows, width), BF16))(conv, second, direct, w_out)


def solution(mesh):
    rows = P(AXES, None)
    in_specs = (rows, P(), P(), rows, rows, P(), P())
    return jax.shard_map(body, mesh=mesh, in_specs=in_specs, out_specs=rows, check_vma=False)
```

```python
import math

import jax
import jax.numpy as jnp
import numpy as np
from jax import lax
from jax.experimental import pallas as pl
from jax.experimental.pallas import tpu as pltpu
from jax.sharding import PartitionSpec as P

AXES = ("blk", "fft")
F32 = jnp.float32
BF16 = jnp.bfloat16
MESSAGE, ROW = 25, 3


def tables(blocks, tok):
    length = 2 * blocks * tok
    half = np.arange(blocks) + 0.5
    ang = 2 * math.pi * np.outer(half, np.arange(2 * blocks)) / (2 * blocks)
    fore = np.concatenate([np.cos(ang), -np.sin(ang)], 0)
    back = np.concatenate([fore[:blocks, :blocks].T, fore[blocks:, :blocks].T], 0) * (2 / length)
    fore[:, blocks:] *= -1
    inner = 2 * math.pi * np.outer(np.arange(tok), np.arange(tok)) / tok
    c, s = np.cos(inner), np.sin(inner)
    inner = np.block([[c, -s], [s, c], [c, s], [-s, c]])
    return jnp.asarray(np.concatenate([fore, inner, back], 1), BF16)


def dot(a, b):
    return jnp.dot(a, b, preferred_element_type=F32)


def first_kernel(twist_ref):
    blocks, tok = twist_ref.shape[0], twist_ref.shape[1] // 2
    k = lax.broadcasted_iota(jnp.int32, (blocks, tok), 0)
    t = lax.broadcasted_iota(jnp.int32, (blocks, tok), 1)
    angle = ((2 * k + 1) * t).astype(F32) * (math.pi / (2 * blocks * tok))
    twist_ref[:, :tok] = jnp.cos(angle)
    twist_ref[:, tok:] = jnp.sin(angle)


def front_kernel(
    _, tok_ref, w_ref, taps_ref, skip_ref, causal_ref, anti_ref,
    send_ref, second_ref, direct_ref, buf, wide,
):
    rows = tok_ref.shape[0]
    channels = causal_ref.shape[1]
    half = channels // 2
    row = lax.broadcasted_iota(jnp.int32, (rows, channels), 0)

    def slab(i):
        return slice(i * channels, (i + 1) * channels)

    def place(a, block):
        buf[...] = block.T
        for c in range(2):
            wide[pl.ds(ROW * (2 * a + c), half, stride=MESSAGE), :] = buf[pl.ds(c, half, stride=2), :]

    def short(i):
        proj = dot(tok_ref[...], w_ref[:, slab(i)]).astype(BF16).astype(F32)
        prior, here, after = [taps_ref[k : k + 1, slab(i)] for k in range(3)]
        up = jnp.where(row == 0, 0.0, pltpu.roll(proj, 1, 0))
        down = jnp.where(row == rows - 1, 0.0, pltpu.roll(proj, rows - 1, 0))
        return prior * up + here * proj + after * down, after * proj[:1], prior * proj[rows - 1 :]

    place(1, causal_ref[...].astype(F32))
    place(2, anti_ref[...].astype(F32))
    first, first_up, first_down = short(0)
    value, value_up, value_down = short(2)
    signal = first * value
    place(0, signal)
    direct_ref[...] = (skip_ref[...] * signal).T
    second, second_up, second_down = short(1)
    second_ref[...] = second.T
    last = rows - 1
    ends = [
        first[:1], value[last:], value[:1], second[last:], second[:1],
        first_up, first_down, value_up, value_down, second_up, second_down,
        skip_ref[...], skip_ref[...],
    ]
    fill = jnp.zeros((rows - len(ends) - 1, channels), F32)
    place(3, jnp.concatenate(ends + [fill, first[last:]], 0))
    for i in range(0, half, 2):
        pair = [wide[pl.ds(MESSAGE * (i + k), 8, stride=ROW), :] for k in range(2)]
        send_ref[8 * i : 8 * i + 16, :] = jnp.concatenate(pair, 0).astype(BF16)


def conv_kernel(got_ref, table_ref, twist_ref, out_ref, buf, wide):
    tok = got_ref.shape[1]
    blocks = got_ref.shape[0] // 8
    cos, sin = twist_ref[:, :tok], twist_ref[:, tok:]
    inner = slice(2 * blocks, 2 * blocks + 2 * tok)
    back = slice(2 * blocks + 2 * tok, 3 * blocks + 2 * tok)
    place = lax.broadcasted_iota(jnp.int32, (blocks, tok), 0)
    lane = lax.broadcasted_iota(jnp.int32, (blocks, tok), 1)
    at_end = (lane == 0) | (lane == tok - 1)

    def left(x, n):
        return pltpu.roll(x, tok - n, 1)

    def take(a, c):
        return wide[pl.ds(ROW * (2 * a + c), blocks, stride=MESSAGE), :]

    def spectrum(b):
        parts = []
        for c in range(2):
            lanes = slice(c * tok, (c + 1) * tok)
            re, im = b[:blocks, lanes], b[blocks:, lanes]
            parts.append(jnp.concatenate([re * cos + im * sin, im * cos - re * sin], 1))
        return [dot(part.astype(BF16), table_ref[: 2 * tok, inner]) for part in parts]

    got = got_ref[...].astype(F32)
    for i in range(blocks):
        wide[pl.ds(MESSAGE * i, 8, stride=ROW), :] = got[8 * i : 8 * i + 8]
    causal = jnp.concatenate([take(1, 0), take(1, 1)], 1)
    anti = jnp.concatenate(
        [jnp.where((place == 0) & (lane == 0), 0.0, take(2, c)) for c in range(2)], 1
    )
    f = spectrum(dot(table_ref[:, : 2 * blocks], jnp.concatenate([causal, anti], 0).astype(BF16)))

    signal, end_signal, end_second, end_skip = [], [], [], []
    for c in range(2):
        ends = take(3, c)
        prior = jnp.where(place == 0, 0.0, pltpu.roll(ends, 1, 0))
        after = jnp.where(place == blocks - 1, 0.0, pltpu.roll(ends, blocks - 1, 0))
        full = ends + left(jnp.where(lane % 2 == 1, after, prior), 6)
        end_signal.append(full * left(full, 2))
        end_second.append(left(full, 4))
        end_skip.append(left(ends, 12))
        signal.append(jnp.where(at_end, end_signal[c], take(0, c)))
    s = spectrum(dot(table_ref[:, :blocks], jnp.concatenate(signal, 1).astype(BF16)))

    real, imag = [], []
    for c in range(2):
        sr, si, fr, fi = s[c][:, :tok], s[c][:, tok:], f[c][:, :tok], f[c][:, tok:]
        y = jnp.concatenate([sr * fr - si * fi, sr * fi + si * fr], 1)
        g = dot(y.astype(BF16), table_ref[2 * tok : 4 * tok, inner])
        re, im = g[:, :tok], g[:, tok:]
        real.append(re * cos - im * sin)
        imag.append(re * sin + im * cos)
    e = jnp.concatenate([jnp.concatenate(real, 1), jnp.concatenate(imag, 1)], 0)
    e = e.astype(BF16)
    rows = [
        jnp.concatenate([table_ref[k : k + tok, back], table_ref[blocks + k : blocks + k + tok, back]], 1)
        for k in range(0, blocks, tok)
    ]
    out = jnp.concatenate([dot(r, e) for r in rows], 0)
    for c in range(2):
        conv = out[:, c * tok : (c + 1) * tok]
        gated = end_second[c] * (conv + end_skip[c] * end_signal[c])
        buf[pl.ds(c, blocks, stride=2), :] = jnp.where(at_end, gated, conv)
    out_ref[...] = buf[...].astype(BF16)


def last_kernel(conv_ref, second_ref, direct_ref, w_ref, out_ref):
    conv = conv_ref[...].astype(F32)
    lane = lax.broadcasted_iota(jnp.int32, conv.shape, 1)
    at_end = (lane == 0) | (lane == conv.shape[1] - 1)
    gated = jnp.where(at_end, conv, second_ref[...] * (conv + direct_ref[...])).astype(BF16)
    out_ref[...] = lax.dot_general(
        gated, w_ref[...], (((0,), (0,)), ((), ())), preferred_element_type=F32
    ).astype(BF16)


def call(kernel, outs, scratch=(), mib=24, cost=0, **specs):
    return pl.pallas_call(
        kernel,
        out_shape=outs,
        scratch_shapes=list(scratch),
        compiler_params=pltpu.CompilerParams(vmem_limit_bytes=mib * 1024 * 1024),
        cost_estimate=pl.CostEstimate(flops=cost, bytes_accessed=0, transcendentals=0) if cost else None,
        **specs,
    )


def exchange(x):
    return lax.all_to_all(x, AXES, split_axis=0, concat_axis=0, tiled=True)


def body(tokens, w_in, conv_taps, causal_taps, anticausal_taps, skip_gain, w_out):
    rows = tokens.shape[0]
    channels, width = w_out.shape
    count = lax.axis_size(AXES)
    shape = jax.ShapeDtypeStruct
    vmem = pltpu.VMEM
    table = tables(count, rows)

    staged = (tokens, w_in, conv_taps, skip_gain[None], causal_taps, anticausal_taps)
    twist = call(first_kernel, shape((count, 2 * rows), F32), cost=2 * 10**9)()
    send, second, direct = call(
        front_kernel,
        [shape((4 * channels, rows), BF16), shape((channels, rows), F32), shape((channels, rows), F32)],
        [vmem((channels, rows), F32), vmem((MESSAGE * (count + 1), rows), F32)],
    )(twist, *staged)
    got = exchange(send.reshape(count, 8, rows)).reshape(send.shape)

    conv = call(
        conv_kernel,
        shape((channels, rows), BF16),
        [vmem((channels, rows), F32), vmem((MESSAGE * (count + 1), rows), F32)],
    )(got, table, twist)
    conv = exchange(conv)
    return call(last_kernel, shape((rows, width), BF16))(conv, second, direct, w_out)


def solution(mesh):
    rows = P(AXES, None)
    in_specs = (rows, P(), P(), rows, rows, P(), P())
    return jax.shard_map(body, mesh=mesh, in_specs=in_specs, out_specs=rows, check_vma=False)
```
